32 devices in a mesh: lo: 4 (over y, x), hi: 8 (over z, core).
Axes of the slice: x: 2, y: 2, z: 4, core: 2. Of those that a mesh axis runs over, the one named last changes fastest.
Arguments:
- coefficients: float32 [2, 32, 8, 32768], P(None, None, None, ('lo', 'hi')), may hold values from -6 to 6
- angle_in: float32 [5, 64, 32768], P(None, None, ('lo', 'hi')), may hold values from -3.140625 to 3.140625
- angle_out: float32 [5, 32, 32768], P(None, None, ('lo', 'hi')), may hold values from -3.140625 to 3.140625
- interp: float32 [5, 32, 64], replicated, may hold values from -0.75 to 0.75
- destination: int32 [32, 1024], P(('lo', 'hi')), may hold values from 0 to 1023, each once within a row
Outputs:
- relaid: float32 [2, 32, 8, 32768], P(None, None, None, ('lo', 'hi'))
The draws below stay inside these ranges and needn't reach their ends.
All inputs are finite; a program needn't handle non-finite values.
Results may differ from the reference program's by a relative error of at most 0.0001.
Values sent between devices are 32-bit elements; how exact they have to be, the bound alone decides.
A program may use at most 128 MiB of HBM per device.

```python
import jax
import jax.numpy as jnp
from jax import lax

R = 32
V = 8
K = 1024
LB_LO = 2
LB_HI = 3
LEVELS = 5
NDEV = 32
BOXES = 32768


def levels(rng, extent, pieces, least, top_value):
    level, own = 1.0, jax.random.fold_in(rng, 6)
    for axis_at, parts in pieces:
        steps = jnp.exp(jax.random.uniform(jax.random.fold_in(own, axis_at), (parts,), jnp.float32, least / len(pieces), top_value / len(pieces)))
        level = level * jnp.repeat(steps, extent[axis_at] // parts).reshape([-1 if axis == axis_at else 1 for axis in range(len(extent))])
    return level


def bell_draw(rng, dims, scale, reach, pieces=(), dtype=jnp.bfloat16):
    entries = jax.random.normal(rng, dims, jnp.float32) * scale
    if len(pieces) > 0:
        entries = levels(rng, dims, pieces, -0.22, 0.18) * entries
    return jnp.clip(entries, min=-reach, max=reach).astype(dtype)


def setup_inputs(seed: int = 0) -> dict:
    keys = jax.random.split(jax.random.key(seed), 6)
    coefficients = bell_draw(keys[0], (2, R, V, BOXES), 1.0, 6.0, ((3, 32),), jnp.float32)
    angle_in = jnp.clip(jax.random.uniform(keys[1], (LEVELS, 2 * R, BOXES), jnp.float32, -3.140625, 3.140625), -3.140625, 3.140625)
    angle_out = jnp.clip(jax.random.uniform(keys[2], (LEVELS, R, BOXES), jnp.float32, -3.140625, 3.140625), -3.140625, 3.140625)
    interp = bell_draw(keys[3], (LEVELS, R, 2 * R), (2 * R) ** -0.5, 0.75, (), jnp.float32)
    destination = jax.vmap(lambda own: jax.random.permutation(own, K))(jax.random.split(keys[4], NDEV)).reshape((NDEV, K)).astype(jnp.int32)
    return dict(coefficients=coefficients, angle_in=angle_in, angle_out=angle_out, interp=interp, destination=destination)


def rotate(real, imag, angle):
    cosine = jnp.cos(angle)
    sine = jnp.sin(angle)
    return real * cosine - imag * sine, real * sine + imag * cosine


def level_step(state, angle_in, angle_out, interp, position):
    ndev = state.shape[3]
    width = state.shape[4]
    half = width // 2
    stride = 2 ** position
    groups = ndev // (2 * stride)
    shaped = state.reshape(2, R, V, groups, 2, stride, width)
    low = shaped[:, :, :, :, 0]
    high = shaped[:, :, :, :, 1]
    phase_in = angle_in.reshape(2 * R, groups, 2, stride, width)
    phase_out = angle_out.reshape(R, groups, 2, stride, width)
    results = []
    for side in range(2):
        joined = jnp.concatenate([low[..., side * half:(side + 1) * half], high[..., side * half:(side + 1) * half]], axis=1)
        wide = jnp.repeat(joined, 2, axis=-1)
        angle = phase_in[:, :, side][:, None]
        yre, yim = rotate(wide[0], wide[1], angle)
        mapped = jnp.einsum("or,crvgsk->covgsk", interp, jnp.stack([yre, yim]), precision=lax.Precision.HIGHEST)
        zre, zim = rotate(mapped[0], mapped[1], phase_out[:, :, side][:, None])
        results.append(jnp.stack([zre, zim]))
    new_state = jnp.stack(results, axis=4)
    return new_state.reshape(2, R, V, ndev, width)


def reference(coefficients, angle_in, angle_out, interp, destination):
    state = coefficients.reshape(2, R, V, NDEV, K)
    step = 0
    for bit in range(LB_LO):
        state = level_step(state, angle_in[step].reshape(2 * R, NDEV, K), angle_out[step].reshape(R, NDEV, K), interp[step], LB_HI + bit)
        step = step + 1
    for bit in range(LB_HI):
        state = level_step(state, angle_in[step].reshape(2 * R, NDEV, K), angle_out[step].reshape(R, NDEV, K), interp[step], bit)
        step = step + 1
    index = jnp.broadcast_to(destination.astype(jnp.int32)[None, None, None], state.shape)
    taken = jnp.take_along_axis(state, index, axis=4)
    piece = K // NDEV
    moved = taken.reshape(2, R, V, NDEV, NDEV, piece)
    moved = jnp.swapaxes(moved, 3, 4)
    return moved.reshape(2, R, V, NDEV * K)
```

```python
import functools

import jax
import jax.numpy as jnp
from jax import lax
from jax.experimental import pallas as pl
from jax.experimental.pallas import tpu as pltpu
from jax.sharding import PartitionSpec as P

MESH = pl.DeviceIdType.MESH
LANES = 128
VC = 2
TILE_BITS = 3


def slot_orders(levels, bits):
    lay = {q: ("k", q) for q in range(bits)}
    orders = []
    for l in range(levels):
        tile = bits - 1 - l % TILE_BITS
        lane = bits - 1 - l
        if l >= TILE_BITS:
            lay[tile], lay[lane] = lay[lane], lay[tile]
        assert lay[tile] == ("k", bits - 1 - l)
        lay[tile] = ("b", l)
        order = {}
        for q, (kind, n) in lay.items():
            order[q] = n + l + 1 if kind == "k" else l - n
        orders.append(order)
    return orders


def to_logical(index, order):
    out = jnp.zeros_like(index)
    for q, p in order.items():
        out = out | (((index >> q) & 1) << p)
    return out


def to_internal(index, order):
    out = jnp.zeros_like(index)
    for q, p in order.items():
        out = out | (((index >> p) & 1) << q)
    return out


def sincos(x):
    y = 0.5 * x
    z = y * y
    s = -1.0 / 39916800
    for c in (1.0 / 362880, -1.0 / 5040, 1.0 / 120, -1.0 / 6, 1.0):
        s = s * z + c
    s = s * y
    c = 1.0 / 479001600
    for k in (-1.0 / 3628800, 1.0 / 40320, -1.0 / 720, 1.0 / 24, -0.5, 1.0):
        c = c * z + k
    return 2.0 * s * c, 1.0 - 2.0 * s * s


def at_tile(l, value, a, b):
    where = l % TILE_BITS
    rest = [a, b]
    rest.insert(where, value)
    return tuple(rest)


def split2(x):
    hi = x.astype(jnp.bfloat16)
    lo = (x - hi.astype(jnp.float32)).astype(jnp.bfloat16)
    return hi, lo


def kernel(
    levels, lo_bits, n_lo, n_hi,
    x_ref, ain_ref, aout_ref, w_ref, dest_ref, out_ref,
    st_ref, got_ref, cos_ref, sin_ref, wk_ref, split_ref, pick_ref, t_ref, r_ref,
    send_sem, recv_sem, tsend_sem, trecv_sem,
):
    chunks = x_ref.shape[0]
    rank = x_ref.shape[-2]
    slots = dest_ref.shape[0]
    bits = slots.bit_length() - 1
    n = n_lo * n_hi
    piece = slots // n
    orders = slot_orders(levels, bits)
    my_lo = lax.axis_index("lo")
    my_hi = lax.axis_index("hi")
    me = my_lo * n_hi + my_hi

    barrier = pltpu.get_barrier_semaphore()

    def greet(i, carry):
        other = lax.rem(me + i, n)
        pl.semaphore_signal(
            barrier, inc=1, device_id=(other // n_hi, lax.rem(other, n_hi)), device_id_type=MESH
        )
        return carry

    lax.fori_loop(1, n, greet, 0)

    def place(l):
        if l < lo_bits:
            axis, own, stride = "lo", my_lo, 2**l
        else:
            axis, own, stride = "hi", my_hi, 2 ** (l - lo_bits)
        side = lax.rem(own // stride, 2)
        return axis, side, own + stride * (1 - 2 * side)

    def state(l, c):
        return x_ref.at[c] if l == 0 else st_ref.at[l - 1, c]

    def exchange(l, c):
        axis, side, partner = place(l)
        where = l % TILE_BITS
        index = (slice(None),) * (2 + where) + (1 - side,)
        device = (partner, my_hi) if axis == "lo" else (my_lo, partner)
        return pltpu.make_async_remote_copy(
            src_ref=state(l, c).at[index],
            dst_ref=got_ref.at[l, c],
            send_sem=send_sem.at[l, c],
            recv_sem=recv_sem.at[l, c],
            device_id=device,
            device_id_type=MESH,
        )

    def prepare(l):
        _, side, _ = place(l)
        w = w_ref[l]
        turned = jnp.concatenate([w[:, rank:], w[:, :rank]], axis=1)
        w = jnp.where(side == 0, w, turned)
        hi, lo = split2(w)
        wk_ref[l] = jnp.concatenate([hi, hi, lo], axis=1)
        rows = 3 * rank
        angle = jnp.concatenate([ain_ref[l], aout_ref[l]], axis=0)
        hi, lo = split2(angle)
        split_ref[0:rows] = hi
        split_ref[rows:2 * rows] = lo
        left = angle - hi.astype(jnp.float32) - lo.astype(jnp.float32)
        split_ref[2 * rows:3 * rows] = left.astype(jnp.bfloat16)

        def body(u, carry):
            wide = 2 * LANES
            index = lax.broadcasted_iota(jnp.int32, (1, wide), 1) + u * wide
            source = to_logical(index, orders[l])
            ids = lax.broadcasted_iota(jnp.int32, (slots, wide), 0)
            hot = jnp.where(ids == source, 1.0, 0.0).astype(jnp.bfloat16)
            got = jnp.dot(split_ref[...], hot, preferred_element_type=jnp.float32)
            got = got[0:rows] + got[rows:2 * rows] + got[2 * rows:3 * rows]
            sine, cosine = sincos(got)
            for half in range(2):
                cols = slice(half * LANES, (half + 1) * LANES)
                for part in range(3):
                    band = slice(part * rank, (part + 1) * rank)
                    sin_ref[l, u * 2 + half, part] = sine[band, cols]
                    cos_ref[l, u * 2 + half, part] = cosine[band, cols]
            return carry

        lax.fori_loop(0, slots // (2 * LANES), body, 0)

    def prepare_pick():
        want = to_internal(dest_ref[...], orders[levels - 1])

        def body(u, carry):
            ids = lax.broadcasted_iota(jnp.int32, (slots, LANES), 1) + u * LANES
            pick_ref[u] = jnp.where(ids == want, 1.0, 0.0).astype(jnp.bfloat16)
            return carry

        lax.fori_loop(0, slots // LANES, body, 0)

    def compute(l, c):
        _, side, _ = place(l)
        src = state(l, c)

        def body(u, carry):
            a, b = u // 2, lax.rem(u, 2)
            kept = at_tile(l, side, a, b)
            kre = [src[(v, 0) + kept] for v in range(VC)]
            kim = [src[(v, 1) + kept] for v in range(VC)]
            gre = [got_ref[l, c, v, 0, a, b] for v in range(VC)]
            gim = [got_ref[l, c, v, 1, a, b] for v in range(VC)]
            columns = []
            tiles = []
            for bit in range(2):
                t9, t8, t7 = at_tile(l, bit, a, b)
                tile = t9 * 4 + t8 * 2 + t7
                tiles.append(tile)
                ck, sk = cos_ref[l, tile, side], sin_ref[l, tile, side]
                cg, sg = cos_ref[l, tile, 1 - side], sin_ref[l, tile, 1 - side]
                for v in range(VC):
                    columns.append(jnp.concatenate(
                        [kre[v] * ck - kim[v] * sk, gre[v] * cg - gim[v] * sg], axis=0))
                    columns.append(jnp.concatenate(
                        [kre[v] * sk + kim[v] * ck, gre[v] * sg + gim[v] * cg], axis=0))
            hi, lo = split2(jnp.concatenate(columns, axis=1))
            stacked = jnp.concatenate([hi, lo, hi], axis=0)
            mapped = jnp.dot(wk_ref[l], stacked, preferred_element_type=jnp.float32)
            for bit in range(2):
                co, so = cos_ref[l, tiles[bit], 2], sin_ref[l, tiles[bit], 2]
                where = at_tile(l, bit, a, b)
                for v in range(VC):
                    at = (bit * VC + v) * 2 * LANES
                    mre = mapped[:, at:at + LANES]
                    mim = mapped[:, at + LANES:at + 2 * LANES]
                    st_ref[(l, c, v, 0) + where] = mre * co - mim * so
                    st_ref[(l, c, v, 1) + where] = mre * so + mim * co
            return carry

        lax.fori_loop(0, 4, body, 0)

    def swap(l, c):
        lane_bit = bits - 1 - l
        shift = 2**lane_bit
        lane = lax.broadcasted_iota(jnp.int32, (rank, LANES), 1)
        clear = ((lane >> lane_bit) & 1) == 0

        def body(u, carry):
            a, b = u // 2, lax.rem(u, 2)
            first, second = at_tile(l, 0, a, b), at_tile(l, 1, a, b)
            for v in range(VC):
                for part in range(2):
                    x = st_ref[(l - 1, c, v, part) + first]
                    y = st_ref[(l - 1, c, v, part) + second]
                    st_ref[(l - 1, c, v, part) + first] = jnp.where(clear, x, pltpu.roll(y, shift, 1))
                    st_ref[(l - 1, c, v, part) + second] = jnp.where(
                        clear, pltpu.roll(x, LANES - shift, 1), y)
            return carry

        lax.fori_loop(0, 4, body, 0)

    def relay(c, i):
        other = lax.rem(me + i, n)
        return pltpu.make_async_remote_copy(
            src_ref=t_ref.at[c, pl.ds(pl.multiple_of(other * piece, piece), piece)],
            dst_ref=r_ref.at[c, pl.ds(pl.multiple_of(me * piece, piece), piece)],
            send_sem=tsend_sem.at[c, i],
            recv_sem=trecv_sem.at[c, i],
            device_id=(other // n_hi, lax.rem(other, n_hi)),
            device_id_type=MESH,
        )

    def relay_in(c, i):
        other = lax.rem(me + n - i, n)
        return pltpu.make_async_remote_copy(
            src_ref=t_ref.at[c, pl.ds(pl.multiple_of(other * piece, piece), piece)],
            dst_ref=r_ref.at[c, pl.ds(pl.multiple_of(other * piece, piece), piece)],
            send_sem=tsend_sem.at[c, i],
            recv_sem=trecv_sem.at[c, i],
            device_id=(other // n_hi, lax.rem(other, n_hi)),
            device_id_type=MESH,
        )

    def gather(c):
        his, los = [], []
        total = None
        for tile in range(slots // LANES):
            where = (tile // 4, tile // 2 % 2, tile % 2)
            block = jnp.concatenate(
                [st_ref[(levels - 1, c, v, part) + where] for v in range(VC) for part in range(2)], axis=0)
            hi, lo = split2(block)
            his.append(jnp.concatenate([hi, lo], axis=0))
        both = jnp.concatenate(his, axis=1)
        split_at = both.shape[0] // 2

        def body(u, carry):
            rows = slots // 4
            at = pl.ds(pl.multiple_of(u * rows, rows), rows)
            hot = jnp.concatenate([pick_ref[t, at] for t in range(slots // LANES)], axis=1)
            got = lax.dot_general(
                hot, both, (((1,), (1,)), ((), ())), preferred_element_type=jnp.float32)
            t_ref[c, at] = got[:, :split_at] + got[:, split_at:]
            return carry

        lax.fori_loop(0, 4, body, 0)
        mine = pl.ds(pl.multiple_of(me * piece, piece), piece)
        r_ref[c, mine] = t_ref[c, mine]

        def send(i, carry):
            relay(c, i).start()
            return carry

        lax.fori_loop(1, n, send, 0)

    def finish(c):
        def wait(i, carry):
            relay_in(c, i).wait_recv()
            return carry

        lax.fori_loop(1, n, wait, 0)
        for g in range(slots // LANES):
            cols = slice(g * LANES, (g + 1) * LANES)
            out_ref[c, :, cols] = r_ref[c, cols].T

    pl.semaphore_wait(barrier, n - 1)
    for c in range(chunks):
        exchange(0, c).start()
    prepared = set()

    def need(l):
        if l < levels and l not in prepared:
            prepared.add(l)
            prepare(l)

    need(0)
    last = levels - 1
    order = sorted(
        ((c, l) for c in range(chunks) for l in range(levels)),
        key=lambda t: (t[0] + t[1] if t[1] < last else t[1] + 2 * t[0], -t[1]),
    )
    for c, l in order:
        need(l)
        exchange(l, c).wait_recv()
        compute(l, c)
        if l < last:
            if l + 1 >= TILE_BITS:
                swap(l + 1, c)
            exchange(l + 1, c).start()
            need(l + 1)
            if l + 1 == last and c == 0:
                prepare_pick()
        else:
            gather(c)
            if c > 0:
                finish(c - 1)
    finish(chunks - 1)
    for c in range(chunks):
        for l in range(levels):
            exchange(l, c).wait_send()

        def sent(i, carry):
            relay(c, i).wait_send()
            return carry

        lax.fori_loop(1, n, sent, 0)


def shards(coefficients, angle_in, angle_out, interp, destination):
    parts, rank, vectors, slots = coefficients.shape
    levels = interp.shape[0]
    n_lo, n_hi = lax.axis_size("lo"), lax.axis_size("hi")
    n = n_lo * n_hi
    chunks = vectors // VC
    x = coefficients.reshape(parts, rank, chunks, VC, 2, 2, 2, LANES)
    x = x.transpose(2, 3, 0, 4, 5, 6, 1, 7)
    rows = VC * parts * rank
    vmem = pl.BlockSpec(memory_space=pltpu.VMEM)
    f32, bf16 = jnp.float32, jnp.bfloat16
    tiles = slots // LANES
    out = pl.pallas_call(
        functools.partial(kernel, levels, n_lo.bit_length() - 1, n_lo, n_hi),
        out_shape=jax.ShapeDtypeStruct((chunks, rows, slots), f32),
        in_specs=[vmem] * 5,
        out_specs=vmem,
        scratch_shapes=[
            pltpu.VMEM((levels, chunks, VC, parts, 2, 2, 2, rank, LANES), f32),
            pltpu.VMEM((levels, chunks, VC, parts, 2, 2, rank, LANES), f32),
            pltpu.VMEM((levels, tiles, 3, rank, LANES), f32),
            pltpu.VMEM((levels, tiles, 3, rank, LANES), f32),
            pltpu.VMEM((levels, rank, 6 * rank), bf16),
            pltpu.VMEM((9 * rank, slots), bf16),
            pltpu.VMEM((tiles, slots, LANES), bf16),
            pltpu.VMEM((chunks, slots, rows), f32),
            pltpu.VMEM((chunks, slots, rows), f32),
            pltpu.SemaphoreType.DMA((levels, chunks)),
            pltpu.SemaphoreType.DMA((levels, chunks)),
            pltpu.SemaphoreType.DMA((chunks, n)),
            pltpu.SemaphoreType.DMA((chunks, n)),
        ],
        compiler_params=pltpu.CompilerParams(
            collective_id=0, has_side_effects=True, vmem_limit_bytes=56 * 1024 * 1024
        ),
    )(x, angle_in, angle_out, interp, destination.reshape(slots, 1))
    out = out.reshape(chunks, VC, parts, rank, slots).transpose(2, 3, 0, 1, 4)
    return out.reshape(parts, rank, vectors, slots)


def solution(mesh):
    placed = (
        P(None, None, None, ("lo", "hi")),
        P(None, None, ("lo", "hi")),
        P(None, None, ("lo", "hi")),
        P(),
        P(("lo", "hi"), None),
    )
    return jax.shard_map(
        shards,
        mesh=mesh,
        in_specs=placed,
        out_specs=P(None, None, None, ("lo", "hi")),
        check_vma=False,
    )
```

```python
import functools

import jax
import jax.numpy as jnp
from jax import lax
from jax.experimental import pallas as pl
from jax.experimental.pallas import tpu as pltpu
from jax.sharding import PartitionSpec as P

MESH = pl.DeviceIdType.MESH
LANES = 128
VC = 1
PAIR = 2
TILE_BITS = 3


def slot_orders(levels, bits):
    lay = {q: ("k", q) for q in range(bits)}
    orders = []
    for l in range(levels):
        tile = bits - 1 - l % TILE_BITS
        lane = bits - 1 - l
        if l >= TILE_BITS:
            lay[tile], lay[lane] = lay[lane], lay[tile]
        assert lay[tile] == ("k", bits - 1 - l)
        lay[tile] = ("b", l)
        order = {}
        for q, (kind, n) in lay.items():
            order[q] = n + l + 1 if kind == "k" else l - n
        orders.append(order)
    return orders


def to_logical(index, order):
    out = jnp.zeros_like(index)
    for q, p in order.items():
        out = out | (((index >> q) & 1) << p)
    return out


def to_internal(index, order):
    out = jnp.zeros_like(index)
    for q, p in order.items():
        out = out | (((index >> p) & 1) << q)
    return out


def sincos(x):
    y = 0.5 * x
    z = y * y
    s = -1.0 / 39916800
    for c in (1.0 / 362880, -1.0 / 5040, 1.0 / 120, -1.0 / 6, 1.0):
        s = s * z + c
    s = s * y
    c = 1.0 / 479001600
    for k in (-1.0 / 3628800, 1.0 / 40320, -1.0 / 720, 1.0 / 24, -0.5, 1.0):
        c = c * z + k
    return 2.0 * s * c, 1.0 - 2.0 * s * s


def at_tile(l, value, a, b):
    where = l % TILE_BITS
    rest = [a, b]
    rest.insert(where, value)
    return tuple(rest)


def split2(x):
    hi = x.astype(jnp.bfloat16)
    lo = (x - hi.astype(jnp.float32)).astype(jnp.bfloat16)
    return hi, lo


def kernel(
    levels, lo_bits, n_lo, n_hi,
    x_ref, ain_ref, aout_ref, w_ref, dest_ref, out_ref,
    xs_ref, os_ref, first_ref, st_ref, got_ref, cos_ref, sin_ref, wk_ref, split_ref, pick_ref, t_ref, r_ref,
    send_sem, recv_sem, tsend_sem, trecv_sem, x_sem, o_sem,
):
    chunks = st_ref.shape[1]
    vectors = chunks * VC
    rank = st_ref.shape[-2]
    slots = dest_ref.shape[1]
    bits = slots.bit_length() - 1
    n = n_lo * n_hi
    piece = slots // n
    orders = slot_orders(levels, bits)
    my_lo = lax.axis_index("lo")
    my_hi = lax.axis_index("hi")
    me = my_lo * n_hi + my_hi

    barrier = pltpu.get_barrier_semaphore()

    def fetch(tile):
        cols = pl.ds(tile * LANES, LANES)
        return pltpu.make_async_copy(x_ref.at[:, cols], xs_ref.at[tile], x_sem.at[tile])

    for tile in range(slots // LANES):
        fetch(tile).start()

    def greet(i, carry):
        other = lax.rem(me + i, n)
        pl.semaphore_signal(
            barrier, inc=1, device_id=(other // n_hi, lax.rem(other, n_hi)), device_id_type=MESH
        )
        return carry

    lax.fori_loop(1, n, greet, 0)

    def place(l):
        if l < lo_bits:
            axis, own, stride = "lo", my_lo, 2**l
        else:
            axis, own, stride = "hi", my_hi, 2 ** (l - lo_bits)
        side = lax.rem(own // stride, 2)
        return axis, side, own + stride * (1 - 2 * side)

    def state(l, c):
        return first_ref.at[c] if l == 0 else st_ref.at[l - 1, c]

    def exchange(l, c):
        axis, side, partner = place(l)
        where = l % TILE_BITS
        index = (slice(None),) * (2 + where) + (1 - side,)
        device = (partner, my_hi) if axis == "lo" else (my_lo, partner)
        return pltpu.make_async_remote_copy(
            src_ref=state(l, c).at[index],
            dst_ref=got_ref.at[l, c],
            send_sem=send_sem.at[l, c],
            recv_sem=recv_sem.at[l, c],
            device_id=device,
            device_id_type=MESH,
        )

    def prepare(l):
        _, side, _ = place(l)
        w = w_ref[l]
        turned = jnp.concatenate([w[:, rank:], w[:, :rank]], axis=1)
        w = jnp.where(side == 0, w, turned)
        hi, lo = split2(w)
        wk_ref[l] = jnp.concatenate([hi, hi, lo], axis=1)
        rows = 3 * rank
        angle = jnp.concatenate([ain_ref[l], aout_ref[l]], axis=0)
        hi, lo = split2(angle)
        split_ref[0:rows] = hi
        split_ref[rows:2 * rows] = lo
        size = min(slots, 2 * LANES << l)

        def body(u, carry):
            wide = 2 * LANES
            if l == 0:
                tiles = (u, u + 4)
                start = u * size
            elif l == 1:
                tiles = (u // 2 + lax.rem(u, 2) * 4, u // 2 + lax.rem(u, 2) * 4 + 2)
                start = u // 2 * size
            else:
                tiles = (2 * u, 2 * u + 1)
                start = 0
            lane = lax.broadcasted_iota(jnp.int32, (1, wide), 1)
            index = jnp.where(lane < LANES, lane + tiles[0] * LANES, lane + (tiles[1] - 1) * LANES)
            source = to_logical(index, orders[l])
            ids = lax.broadcasted_iota(jnp.int32, (size, wide), 0) + start
            hot = jnp.where(ids == source, 1.0, 0.0).astype(jnp.bfloat16)
            if size == slots:
                left = split_ref[...]
            else:
                left = split_ref[:, pl.ds(pl.multiple_of(start, size), size)]
            got = jnp.dot(left, hot, preferred_element_type=jnp.float32)
            got = got[0:rows] + got[rows:2 * rows]
            sine, cosine = sincos(got)
            for half in range(2):
                cols = slice(half * LANES, (half + 1) * LANES)
                for part in range(3):
                    band = slice(part * rank, (part + 1) * rank)
                    sin_ref[l, tiles[half], part] = sine[band, cols]
                    cos_ref[l, tiles[half], part] = cosine[band, cols]
            return carry

        lax.fori_loop(0, slots // (2 * LANES), body, 0)

    def prepare_pick():
        ids = lax.broadcasted_iota(jnp.int32, (LANES, LANES), 1).astype(jnp.float32)

        for g in range(slots // LANES):
            rows = slice(g * LANES, (g + 1) * LANES)
            want = to_internal(dest_ref[:, rows], orders[levels - 1]).astype(jnp.float32)
            want = jnp.broadcast_to(want, (LANES, LANES)).T

            for u in range(slots // LANES):
                hot = jnp.where(ids + float(u * LANES) == want, 1.0, 0.0)
                pick_ref[u, rows] = hot.astype(jnp.bfloat16)

    def load_first(c):
        for v in range(VC):
            for part in range(2):
                rows = pl.ds(part * rank * vectors + c * VC + v, rank, stride=vectors)
                for tile in range(slots // LANES):
                    first_ref[c, v, part, tile // 4, tile // 2 % 2, tile % 2] = xs_ref[tile, rows, :]

    def compute(l, c):
        _, side, _ = place(l)
        src = state(l, c)

        def body(u, carry):
            a, b = u // 2, lax.rem(u, 2)
            kept = at_tile(l, side, a, b)
            kre = [src[(v, 0) + kept] for v in range(VC)]
            kim = [src[(v, 1) + kept] for v in range(VC)]
            gre = [got_ref[l, c, v, 0, a, b] for v in range(VC)]
            gim = [got_ref[l, c, v, 1, a, b] for v in range(VC)]
            columns = []
            tiles = []
            for bit in range(2):
                t9, t8, t7 = at_tile(l, bit, a, b)
                tile = t9 * 4 + t8 * 2 + t7
                tiles.append(tile)
                ck, sk = cos_ref[l, tile, side], sin_ref[l, tile, side]
                cg, sg = cos_ref[l, tile, 1 - side], sin_ref[l, tile, 1 - side]
                for v in range(VC):
                    columns.append(jnp.concatenate(
                        [kre[v] * ck - kim[v] * sk, gre[v] * cg - gim[v] * sg], axis=0))
                    columns.append(jnp.concatenate(
                        [kre[v] * sk + kim[v] * ck, gre[v] * sg + gim[v] * cg], axis=0))
            hi, lo = split2(jnp.concatenate(columns, axis=1))
            stacked = jnp.concatenate([hi, lo, hi], axis=0)
            mapped = jnp.dot(wk_ref[l], stacked, preferred_element_type=jnp.float32)
            for bit in range(2):
                co, so = cos_ref[l, tiles[bit], 2], sin_ref[l, tiles[bit], 2]
                where = at_tile(l, bit, a, b)
                for v in range(VC):
                    at = (bit * VC + v) * 2 * LANES
                    mre = mapped[:, at:at + LANES]
                    mim = mapped[:, at + LANES:at + 2 * LANES]
                    st_ref[(l, c, v, 0) + where] = mre * co - mim * so
                    st_ref[(l, c, v, 1) + where] = mre * so + mim * co
            return carry

        lax.fori_loop(0, 4, body, 0)

    def swap(l, c):
        lane_bit = bits - 1 - l
        shift = 2**lane_bit
        lane = lax.broadcasted_iota(jnp.int32, (rank, LANES), 1)
        clear = ((lane >> lane_bit) & 1) == 0

        def body(u, carry):
            a, b = u // 2, lax.rem(u, 2)
            first, second = at_tile(l, 0, a, b), at_tile(l, 1, a, b)
            for v in range(VC):
                for part in range(2):
                    x = st_ref[(l - 1, c, v, part) + first]
                    y = st_ref[(l - 1, c, v, part) + second]
                    st_ref[(l - 1, c, v, part) + first] = jnp.where(clear, x, pltpu.roll(y, shift, 1))
                    st_ref[(l - 1, c, v, part) + second] = jnp.where(
                        clear, pltpu.roll(x, LANES - shift, 1), y)
            return carry

        lax.fori_loop(0, 4, body, 0)

    def offsets(i):
        step = i // n_lo
        off_hi = n_hi // 2 + (step + 1) // 2 * (2 * lax.rem(step, 2) - 1)
        return lax.rem(lax.rem(i, n_lo) + 1, n_lo), lax.rem(off_hi, n_hi)

    def relay(c, i):
        off_lo, off_hi = offsets(i)
        to_lo, to_hi = lax.rem(my_lo + off_lo, n_lo), lax.rem(my_hi + off_hi, n_hi)
        other = to_lo * n_hi + to_hi
        return pltpu.make_async_remote_copy(
            src_ref=t_ref.at[c, pl.ds(pl.multiple_of(other * piece, piece), piece)],
            dst_ref=r_ref.at[c, pl.ds(pl.multiple_of(me * piece, piece), piece)],
            send_sem=tsend_sem.at[c, i],
            recv_sem=trecv_sem.at[c, i],
            device_id=(to_lo, to_hi),
            device_id_type=MESH,
        )

    def relay_in(c, i):
        off_lo, off_hi = offsets(i)
        to_lo = lax.rem(my_lo + n_lo - off_lo, n_lo)
        to_hi = lax.rem(my_hi + n_hi - off_hi, n_hi)
        other = to_lo * n_hi + to_hi
        return pltpu.make_async_remote_copy(
            src_ref=t_ref.at[c, pl.ds(pl.multiple_of(other * piece, piece), piece)],
            dst_ref=r_ref.at[c, pl.ds(pl.multiple_of(other * piece, piece), piece)],
            send_sem=tsend_sem.at[c, i],
            recv_sem=trecv_sem.at[c, i],
            device_id=(to_lo, to_hi),
            device_id_type=MESH,
        )

    def gather(c):
        his, los = [], []
        total = None
        for tile in range(slots // LANES):
            where = (tile // 4, tile // 2 % 2, tile % 2)
            block = jnp.concatenate(
                [st_ref[(levels - 1, PAIR * c + v, 0, part) + where] for v in range(PAIR) for part in range(2)], axis=0)
            hi, lo = split2(block)
            his.append(jnp.concatenate([hi, lo], axis=0))
        both = jnp.concatenate(his, axis=1)
        split_at = both.shape[0] // 2

        def body(u, carry):
            rows = slots // 4
            at = pl.ds(pl.multiple_of(u * rows, rows), rows)
            hot = jnp.concatenate([pick_ref[t, at] for t in range(slots // LANES)], axis=1)
            got = lax.dot_general(
                hot, both, (((1,), (1,)), ((), ())), preferred_element_type=jnp.float32)
            t_ref[c, at] = got[:, :split_at] + got[:, split_at:]
            return carry

        lax.fori_loop(0, 4, body, 0)
        mine = pl.ds(pl.multiple_of(me * piece, piece), piece)
        r_ref[c, mine] = t_ref[c, mine]

        def send(i, carry):
            relay(c, i).start()
            return carry

        lax.fori_loop(0, n - 1, send, 0)

    def put(tile):
        cols = pl.ds(tile * LANES, LANES)
        return pltpu.make_async_copy(os_ref.at[tile], out_ref.at[:, cols], o_sem.at[tile])

    def finish(c):
        def wait(i, carry):
            relay_in(c, i).wait_recv()
            return carry

        lax.fori_loop(0, n - 1, wait, 0)
        for g in range(slots // LANES):
            cols = slice(g * LANES, (g + 1) * LANES)
            block = r_ref[c, cols].T
            for v in range(PAIR):
                for part in range(2):
                    at = (v * 2 + part) * rank
                    rows = pl.ds(part * rank * vectors + c * PAIR + v, rank, stride=vectors)
                    os_ref[g, rows, :] = block[at:at + rank]
            if c == chunks // PAIR - 1:
                put(g).start()

    for tile in range(slots // LANES):
        fetch(tile).wait()
    load_first(0)
    pl.semaphore_wait(barrier, n - 1)
    for c in range(chunks):
        if c > 0:
            load_first(c)
        exchange(0, c).start()
    prepared = set()

    def need(l):
        if l < levels and l not in prepared:
            prepared.add(l)
            prepare(l)

    need(0)
    last = levels - 1
    order = sorted(
        ((c, l) for c in range(chunks) for l in range(levels)),
        key=lambda t: (t[0] + t[1] if t[1] < last else t[1] + 2 * t[0] + 1.5, -t[1]),
    )
    for c, l in order:
        need(l)
        exchange(l, c).wait_recv()
        compute(l, c)
        if l < last:
            if l + 1 >= TILE_BITS:
                swap(l + 1, c)
            exchange(l + 1, c).start()
            need(l + 1)
            if l + 1 == last and c == 0:
                prepare_pick()
        elif c % PAIR == PAIR - 1:
            gather(c // PAIR)
            if c >= PAIR:
                finish(c // PAIR - 1)
    finish(chunks // PAIR - 1)
    for tile in range(slots // LANES):
        put(tile).wait()
    for c in range(chunks):
        for l in range(levels):
            exchange(l, c).wait_send()
    for c in range(chunks // PAIR):

        def sent(i, carry):
            relay(c, i).wait_send()
            return carry

        lax.fori_loop(0, n - 1, sent, 0)


def shards(coefficients, angle_in, angle_out, interp, destination):
    parts, rank, vectors, slots = coefficients.shape
    levels = interp.shape[0]
    n_lo, n_hi = lax.axis_size("lo"), lax.axis_size("hi")
    n = n_lo * n_hi
    chunks = vectors // VC
    pairs = vectors // PAIR
    rows = PAIR * parts * rank
    vmem = pl.BlockSpec(memory_space=pltpu.VMEM)
    f32, bf16 = jnp.float32, jnp.bfloat16
    tiles = slots // LANES
    out = pl.pallas_call(
        functools.partial(kernel, levels, n_lo.bit_length() - 1, n_lo, n_hi),
        out_shape=jax.ShapeDtypeStruct((parts * rank * vectors, slots), f32),
        in_specs=[pl.BlockSpec(memory_space=pl.ANY)] + [vmem] * 4,
        out_specs=pl.BlockSpec(memory_space=pl.ANY),
        scratch_shapes=[
            pltpu.VMEM((tiles, parts * rank * vectors, LANES), f32),
            pltpu.VMEM((tiles, parts * rank * vectors, LANES), f32),
            pltpu.VMEM((chunks, VC, parts, 2, 2, 2, rank, LANES), f32),
            pltpu.VMEM((levels, chunks, VC, parts, 2, 2, 2, rank, LANES), f32),
            pltpu.VMEM((levels, chunks, VC, parts, 2, 2, rank, LANES), f32),
            pltpu.VMEM((levels, tiles, 3, rank, LANES), f32),
            pltpu.VMEM((levels, tiles, 3, rank, LANES), f32),
            pltpu.VMEM((levels, rank, 6 * rank), bf16),
            pltpu.VMEM((6 * rank, slots), bf16),
            pltpu.VMEM((tiles, slots, LANES), bf16),
            pltpu.VMEM((pairs, slots, rows), f32),
            pltpu.VMEM((pairs, slots, rows), f32),
            pltpu.SemaphoreType.DMA((levels, chunks)),
            pltpu.SemaphoreType.DMA((levels, chunks)),
            pltpu.SemaphoreType.DMA((pairs, n)),
            pltpu.SemaphoreType.DMA((pairs, n)),
            pltpu.SemaphoreType.DMA((tiles,)),
            pltpu.SemaphoreType.DMA((tiles,)),
        ],
        compiler_params=pltpu.CompilerParams(
            collective_id=0, has_side_effects=True, vmem_limit_bytes=56 * 1024 * 1024
        ),
    )(coefficients.reshape(-1, slots), angle_in, angle_out, interp, destination)
    return out.reshape(parts, rank, vectors, slots)


def solution(mesh):
    placed = (
        P(None, None, None, ("lo", "hi")),
        P(None, None, ("lo", "hi")),
        P(None, None, ("lo", "hi")),
        P(),
        P(("lo", "hi"), None),
    )
    return jax.shard_map(
        shards,
        mesh=mesh,
        in_specs=placed,
        out_specs=P(None, None, None, ("lo", "hi")),
        check_vma=False,
    )
```

```python
import functools

import jax
import jax.numpy as jnp
from jax import lax
from jax.experimental import pallas as pl
from jax.experimental.pallas import tpu as pltpu
from jax.sharding import PartitionSpec as P

MESH = pl.DeviceIdType.MESH
LANES = 128
VC = 1
PAIR = 2
AHEAD = 4
TILE_BITS = 3


def slot_orders(levels, bits):
    lay = {q: ("k", q) for q in range(bits)}
    orders = []
    for l in range(levels):
        tile = bits - 1 - l % TILE_BITS
        lane = bits - 1 - l
        if l >= TILE_BITS:
            lay[tile], lay[lane] = lay[lane], lay[tile]
        assert lay[tile] == ("k", bits - 1 - l)
        lay[tile] = ("b", l)
        order = {}
        for q, (kind, n) in lay.items():
            order[q] = n + l + 1 if kind == "k" else l - n
        orders.append(order)
    return orders


def to_logical(index, order):
    out = jnp.zeros_like(index)
    for q, p in order.items():
        out = out | (((index >> q) & 1) << p)
    return out


def to_internal(index, order):
    out = jnp.zeros_like(index)
    for q, p in order.items():
        out = out | (((index >> p) & 1) << q)
    return out


def sincos(x):
    y = 0.5 * x
    z = y * y
    s = -1.0 / 39916800
    for c in (1.0 / 362880, -1.0 / 5040, 1.0 / 120, -1.0 / 6, 1.0):
        s = s * z + c
    s = s * y
    c = 1.0 / 479001600
    for k in (-1.0 / 3628800, 1.0 / 40320, -1.0 / 720, 1.0 / 24, -0.5, 1.0):
        c = c * z + k
    return 2.0 * s * c, 1.0 - 2.0 * s * s


def at_tile(l, value, a, b):
    where = l % TILE_BITS
    rest = [a, b]
    rest.insert(where, value)
    return tuple(rest)


def split2(x):
    hi = x.astype(jnp.bfloat16)
    lo = (x - hi.astype(jnp.float32)).astype(jnp.bfloat16)
    return hi, lo


def kernel(
    levels, lo_bits, n_lo, n_hi,
    x_ref, ain_hbm, aout_hbm, w_ref, dest_ref, out_ref,
    ain_ref, aout_ref, xs_ref, os_ref, first_ref, st_ref, got_ref, cos_ref, sin_ref, wk_ref, split_ref, pick_ref, t_ref, r_ref,
    send_sem, recv_sem, tsend_sem, trecv_sem, x_sem, o_sem, a_sem,
):
    chunks = st_ref.shape[1]
    vectors = chunks * VC
    rank = st_ref.shape[-2]
    slots = dest_ref.shape[1]
    bits = slots.bit_length() - 1
    n = n_lo * n_hi
    piece = slots // n
    orders = slot_orders(levels, bits)
    my_lo = lax.axis_index("lo")
    my_hi = lax.axis_index("hi")
    me = my_lo * n_hi + my_hi

    barrier = pltpu.get_barrier_semaphore()

    def fetch(tile):
        cols = pl.ds(tile * LANES, LANES)
        return pltpu.make_async_copy(x_ref.at[:, cols], xs_ref.at[tile], x_sem.at[tile])

    for tile in range(slots // LANES):
        fetch(tile).start()

    def fetch_angles(l):
        return (
            pltpu.make_async_copy(ain_hbm.at[l], ain_ref.at[l], a_sem.at[0, l]),
            pltpu.make_async_copy(aout_hbm.at[l], aout_ref.at[l], a_sem.at[1, l]),
        )

    for l in range(levels):
        for copy in fetch_angles(l):
            copy.start()

    def greet(i, carry):
        other = lax.rem(me + i, n)
        pl.semaphore_signal(
            barrier, inc=1, device_id=(other // n_hi, lax.rem(other, n_hi)), device_id_type=MESH
        )
        return carry

    lax.fori_loop(1, n, greet, 0)

    def place(l):
        if l < lo_bits:
            axis, own, stride = "lo", my_lo, 2**l
        else:
            axis, own, stride = "hi", my_hi, 2 ** (l - lo_bits)
        side = lax.rem(own // stride, 2)
        return axis, side, own + stride * (1 - 2 * side)

    def state(l, c):
        return first_ref.at[c] if l == 0 else st_ref.at[l - 1, c]

    def exchange(l, c):
        axis, side, partner = place(l)
        where = l % TILE_BITS
        index = (slice(None),) * (2 + where) + (1 - side,)
        device = (partner, my_hi) if axis == "lo" else (my_lo, partner)
        return pltpu.make_async_remote_copy(
            src_ref=state(l, c).at[index],
            dst_ref=got_ref.at[l, c],
            send_sem=send_sem.at[l, c],
            recv_sem=recv_sem.at[l, c],
            device_id=device,
            device_id_type=MESH,
        )

    def prepare(l):
        _, side, _ = place(l)
        w = w_ref[l]
        turned = jnp.concatenate([w[:, rank:], w[:, :rank]], axis=1)
        w = jnp.where(side == 0, w, turned)
        hi, lo = split2(w)
        wk_ref[l] = jnp.concatenate([hi, hi, lo], axis=1)
        rows = 3 * rank
        for copy in fetch_angles(l):
            copy.wait()
        angle = jnp.concatenate([ain_ref[l], aout_ref[l]], axis=0)
        hi, lo = split2(angle)
        split_ref[0:rows] = hi
        split_ref[rows:2 * rows] = lo
        size = min(slots, 2 * LANES << l)

        def body(u, carry):
            wide = 2 * LANES
            if l == 0:
                tiles = (u, u + 4)
                start = u * size
            elif l == 1:
                tiles = (u // 2 + lax.rem(u, 2) * 4, u // 2 + lax.rem(u, 2) * 4 + 2)
                start = u // 2 * size
            else:
                tiles = (2 * u, 2 * u + 1)
                start = 0
            lane = lax.broadcasted_iota(jnp.int32, (1, wide), 1)
            index = jnp.where(lane < LANES, lane + tiles[0] * LANES, lane + (tiles[1] - 1) * LANES)
            source = to_logical(index, orders[l])
            ids = lax.broadcasted_iota(jnp.int32, (size, wide), 0) + start
            hot = jnp.where(ids == source, 1.0, 0.0).astype(jnp.bfloat16)
            if size == slots:
                left = split_ref[...]
            else:
                left = split_ref[:, pl.ds(pl.multiple_of(start, size), size)]
            got = jnp.dot(left, hot, preferred_element_type=jnp.float32)
            got = got[0:rows] + got[rows:2 * rows]
            sine, cosine = sincos(got)
            for half in range(2):
                cols = slice(half * LANES, (half + 1) * LANES)
                for part in range(3):
                    band = slice(part * rank, (part + 1) * rank)
                    sin_ref[l, tiles[half], part] = sine[band, cols]
                    cos_ref[l, tiles[half], part] = cosine[band, cols]
            return carry

        lax.fori_loop(0, slots // (2 * LANES), body, 0)

    def prepare_pick():
        ids = lax.broadcasted_iota(jnp.int32, (LANES, LANES), 1).astype(jnp.float32)

        for g in range(slots // LANES):
            rows = slice(g * LANES, (g + 1) * LANES)
            want = to_internal(dest_ref[:, rows], orders[levels - 1]).astype(jnp.float32)
            want = jnp.broadcast_to(want, (LANES, LANES)).T

            for u in range(slots // LANES):
                hot = jnp.where(ids + float(u * LANES) == want, 1.0, 0.0)
                pick_ref[u, rows] = hot.astype(jnp.bfloat16)

    def load_first(c):
        for v in range(VC):
            for part in range(2):
                rows = pl.ds(part * rank * vectors + c * VC + v, rank, stride=vectors)
                for tile in range(slots // LANES):
                    first_ref[c, v, part, tile // 4, tile // 2 % 2, tile % 2] = xs_ref[tile, rows, :]

    def compute(l, c):
        _, side, _ = place(l)
        src = state(l, c)

        def body(u, carry):
            a, b = u // 2, lax.rem(u, 2)
            kept = at_tile(l, side, a, b)
            kre = [src[(v, 0) + kept] for v in range(VC)]
            kim = [src[(v, 1) + kept] for v in range(VC)]
            gre = [got_ref[l, c, v, 0, a, b] for v in range(VC)]
            gim = [got_ref[l, c, v, 1, a, b] for v in range(VC)]
            columns = []
            tiles = []
            for bit in range(2):
                t9, t8, t7 = at_tile(l, bit, a, b)
                tile = t9 * 4 + t8 * 2 + t7
                tiles.append(tile)
                ck, sk = cos_ref[l, tile, side], sin_ref[l, tile, side]
                cg, sg = cos_ref[l, tile, 1 - side], sin_ref[l, tile, 1 - side]
                for v in range(VC):
                    columns.append(jnp.concatenate(
                        [kre[v] * ck - kim[v] * sk, gre[v] * cg - gim[v] * sg], axis=0))
                    columns.append(jnp.concatenate(
                        [kre[v] * sk + kim[v] * ck, gre[v] * sg + gim[v] * cg], axis=0))
            hi, lo = split2(jnp.concatenate(columns, axis=1))
            stacked = jnp.concatenate([hi, lo, hi], axis=0)
            mapped = jnp.dot(wk_ref[l], stacked, preferred_element_type=jnp.float32)
            for bit in range(2):
                co, so = cos_ref[l, tiles[bit], 2], sin_ref[l, tiles[bit], 2]
                where = at_tile(l, bit, a, b)
                for v in range(VC):
                    at = (bit * VC + v) * 2 * LANES
                    mre = mapped[:, at:at + LANES]
                    mim = mapped[:, at + LANES:at + 2 * LANES]
                    st_ref[(l, c, v, 0) + where] = mre * co - mim * so
                    st_ref[(l, c, v, 1) + where] = mre * so + mim * co
            return carry

        lax.fori_loop(0, 4, body, 0, unroll=2)

    def swap(l, c):
        lane_bit = bits - 1 - l
        shift = 2**lane_bit
        lane = lax.broadcasted_iota(jnp.int32, (rank, LANES), 1)
        clear = ((lane >> lane_bit) & 1) == 0

        def body(u, carry):
            a, b = u // 2, lax.rem(u, 2)
            first, second = at_tile(l, 0, a, b), at_tile(l, 1, a, b)
            for v in range(VC):
                for part in range(2):
                    x = st_ref[(l - 1, c, v, part) + first]
                    y = st_ref[(l - 1, c, v, part) + second]
                    st_ref[(l - 1, c, v, part) + first] = jnp.where(clear, x, pltpu.roll(y, shift, 1))
                    st_ref[(l - 1, c, v, part) + second] = jnp.where(
                        clear, pltpu.roll(x, LANES - shift, 1), y)
            return carry

        lax.fori_loop(0, 4, body, 0)

    def offsets(i):
        step = i // n_lo
        off_hi = n_hi // 2 + (step + 1) // 2 * (2 * lax.rem(step, 2) - 1)
        return lax.rem(lax.rem(i, n_lo) + 1, n_lo), lax.rem(off_hi, n_hi)

    def relay(c, i):
        off_lo, off_hi = offsets(i)
        to_lo, to_hi = lax.rem(my_lo + off_lo, n_lo), lax.rem(my_hi + off_hi, n_hi)
        other = to_lo * n_hi + to_hi
        return pltpu.make_async_remote_copy(
            src_ref=t_ref.at[c, pl.ds(pl.multiple_of(other * piece, piece), piece)],
            dst_ref=r_ref.at[c, pl.ds(pl.multiple_of(me * piece, piece), piece)],
            send_sem=tsend_sem.at[c, i],
            recv_sem=trecv_sem.at[c, i],
            device_id=(to_lo, to_hi),
            device_id_type=MESH,
        )

    def relay_in(c, i):
        off_lo, off_hi = offsets(i)
        to_lo = lax.rem(my_lo + n_lo - off_lo, n_lo)
        to_hi = lax.rem(my_hi + n_hi - off_hi, n_hi)
        other = to_lo * n_hi + to_hi
        return pltpu.make_async_remote_copy(
            src_ref=t_ref.at[c, pl.ds(pl.multiple_of(other * piece, piece), piece)],
            dst_ref=r_ref.at[c, pl.ds(pl.multiple_of(other * piece, piece), piece)],
            send_sem=tsend_sem.at[c, i],
            recv_sem=trecv_sem.at[c, i],
            device_id=(to_lo, to_hi),
            device_id_type=MESH,
        )

    def gather(c):
        his, los = [], []
        total = None
        for tile in range(slots // LANES):
            where = (tile // 4, tile // 2 % 2, tile % 2)
            block = jnp.concatenate(
                [st_ref[(levels - 1, PAIR * c + v, 0, part) + where] for v in range(PAIR) for part in range(2)], axis=0)
            hi, lo = split2(block)
            his.append(jnp.concatenate([hi, lo], axis=0))
        both = jnp.concatenate(his, axis=1)
        split_at = both.shape[0] // 2

        def body(u, carry):
            rows = slots // 4
            at = pl.ds(pl.multiple_of(u * rows, rows), rows)
            hot = jnp.concatenate([pick_ref[t, at] for t in range(slots // LANES)], axis=1)
            got = lax.dot_general(
                hot, both, (((1,), (1,)), ((), ())), preferred_element_type=jnp.float32)
            t_ref[c, at] = got[:, :split_at] + got[:, split_at:]
            return carry

        lax.fori_loop(0, 4, body, 0)
        mine = pl.ds(pl.multiple_of(me * piece, piece), piece)
        r_ref[c, mine] = t_ref[c, mine]

        def send(i, carry):
            relay(c, i).start()
            return carry

        lax.fori_loop(0, n - 1, send, 0)

    def put(tile):
        cols = pl.ds(tile * LANES, LANES)
        return pltpu.make_async_copy(os_ref.at[tile], out_ref.at[:, cols], o_sem.at[tile])

    def finish(c):
        def wait(i, carry):
            relay_in(c, i).wait_recv()
            return carry

        lax.fori_loop(0, n - 1, wait, 0)
        for g in range(slots // LANES):
            cols = slice(g * LANES, (g + 1) * LANES)
            block = r_ref[c, cols].T
            for v in range(PAIR):
                for part in range(2):
                    at = (v * 2 + part) * rank
                    rows = pl.ds(part * rank * vectors + c * PAIR + v, rank, stride=vectors)
                    os_ref[g, rows, :] = block[at:at + rank]
            if c == chunks // PAIR - 1:
                put(g).start()

    for tile in range(slots // LANES):
        fetch(tile).wait()
    load_first(0)
    pl.semaphore_wait(barrier, n - 1)
    exchange(0, 0).start()
    for c in range(1, AHEAD):
        load_first(c)
        exchange(0, c).start()
    prepared = set()

    def need(l):
        if l < levels and l not in prepared:
            prepared.add(l)
            prepare(l)

    need(0)
    last = levels - 1
    order = sorted(
        ((c, l) for c in range(chunks) for l in range(levels)),
        key=lambda t: (t[0] + t[1] if t[1] < last else t[1] + 2 * t[0] + 1.5, -t[1]),
    )
    for c, l in order:
        need(l)
        exchange(l, c).wait_recv()
        compute(l, c)
        if l == 0 and c + AHEAD < chunks:
            load_first(c + AHEAD)
            exchange(0, c + AHEAD).start()
        if l < last:
            if l + 1 >= TILE_BITS:
                swap(l + 1, c)
            exchange(l + 1, c).start()
            need(l + 1)
            if l + 1 == last and c == 0:
                prepare_pick()
        elif c % PAIR == PAIR - 1:
            gather(c // PAIR)
    for c in range(chunks // PAIR):
        finish(c)
    for tile in range(slots // LANES):
        put(tile).wait()
    for c in range(chunks):
        for l in range(levels):
            exchange(l, c).wait_send()
    for c in range(chunks // PAIR):

        def sent(i, carry):
            relay(c, i).wait_send()
            return carry

        lax.fori_loop(0, n - 1, sent, 0)


def shards(coefficients, angle_in, angle_out, interp, destination):
    parts, rank, vectors, slots = coefficients.shape
    levels = interp.shape[0]
    n_lo, n_hi = lax.axis_size("lo"), lax.axis_size("hi")
    n = n_lo * n_hi
    chunks = vectors // VC
    pairs = vectors // PAIR
    rows = PAIR * parts * rank
    vmem = pl.BlockSpec(memory_space=pltpu.VMEM)
    f32, bf16 = jnp.float32, jnp.bfloat16
    tiles = slots // LANES
    out = pl.pallas_call(
        functools.partial(kernel, levels, n_lo.bit_length() - 1, n_lo, n_hi),
        out_shape=jax.ShapeDtypeStruct((parts * rank * vectors, slots), f32),
        in_specs=[pl.BlockSpec(memory_space=pl.ANY)] * 3 + [vmem] * 2,
        out_specs=pl.BlockSpec(memory_space=pl.ANY),
        scratch_shapes=[
            pltpu.VMEM((levels, 2 * rank, slots), f32),
            pltpu.VMEM((levels, rank, slots), f32),
            pltpu.VMEM((tiles, parts * rank * vectors, LANES), f32),
            pltpu.VMEM((tiles, parts * rank * vectors, LANES), f32),
            pltpu.VMEM((chunks, VC, parts, 2, 2, 2, rank, LANES), f32),
            pltpu.VMEM((levels, chunks, VC, parts, 2, 2, 2, rank, LANES), f32),
            pltpu.VMEM((levels, chunks, VC, parts, 2, 2, rank, LANES), f32),
            pltpu.VMEM((levels, tiles, 3, rank, LANES), f32),
            pltpu.VMEM((levels, tiles, 3, rank, LANES), f32),
            pltpu.VMEM((levels, rank, 6 * rank), bf16),
            pltpu.VMEM((6 * rank, slots), bf16),
            pltpu.VMEM((tiles, slots, LANES), bf16),
            pltpu.VMEM((pairs, slots, rows), f32),
            pltpu.VMEM((pairs, slots, rows), f32),
            pltpu.SemaphoreType.DMA((levels, chunks)),
            pltpu.SemaphoreType.DMA((levels, chunks)),
            pltpu.SemaphoreType.DMA((pairs, n)),
            pltpu.SemaphoreType.DMA((pairs, n)),
            pltpu.SemaphoreType.DMA((tiles,)),
            pltpu.SemaphoreType.DMA((tiles,)),
            pltpu.SemaphoreType.DMA((2, levels)),
        ],
        compiler_params=pltpu.CompilerParams(
            collective_id=0, has_side_effects=True, vmem_limit_bytes=56 * 1024 * 1024
        ),
    )(coefficients.reshape(-1, slots), angle_in, angle_out, interp, destination)
    return out.reshape(parts, rank, vectors, slots)


def solution(mesh):
    placed = (
        P(None, None, None, ("lo", "hi")),
        P(None, None, ("lo", "hi")),
        P(None, None, ("lo", "hi")),
        P(),
        P(("lo", "hi"), None),
    )
    return jax.shard_map(
        shards,
        mesh=mesh,
        in_specs=placed,
        out_specs=P(None, None, None, ("lo", "hi")),
        check_vma=False,
    )
```

```python
import functools

import jax
import jax.numpy as jnp
from jax import lax
from jax.experimental import pallas as pl
from jax.experimental.pallas import tpu as pltpu
from jax.sharding import PartitionSpec as P

MESH = pl.DeviceIdType.MESH
LANES = 128
VC = 1
PAIR = 2
AHEAD = 4
TILE_BITS = 3


def slot_orders(levels, bits):
    lay = {q: ("k", q) for q in range(bits)}
    orders = []
    for l in range(levels):
        tile = bits - 1 - l % TILE_BITS
        lane = bits - 1 - l
        if l >= TILE_BITS:
            lay[tile], lay[lane] = lay[lane], lay[tile]
        assert lay[tile] == ("k", bits - 1 - l)
        lay[tile] = ("b", l)
        order = {}
        for q, (kind, n) in lay.items():
            order[q] = n + l + 1 if kind == "k" else l - n
        orders.append(order)
    return orders


def to_logical(index, order):
    out = jnp.zeros_like(index)
    for q, p in order.items():
        out = out | (((index >> q) & 1) << p)
    return out


def to_internal(index, order):
    out = jnp.zeros_like(index)
    for q, p in order.items():
        out = out | (((index >> p) & 1) << q)
    return out


def sincos(x):
    y = 0.5 * x
    z = y * y
    s = -1.0 / 39916800
    for c in (1.0 / 362880, -1.0 / 5040, 1.0 / 120, -1.0 / 6, 1.0):
        s = s * z + c
    s = s * y
    c = 1.0 / 479001600
    for k in (-1.0 / 3628800, 1.0 / 40320, -1.0 / 720, 1.0 / 24, -0.5, 1.0):
        c = c * z + k
    return 2.0 * s * c, 1.0 - 2.0 * s * s


def at_tile(l, value, a, b):
    where = l % TILE_BITS
    rest = [a, b]
    rest.insert(where, value)
    return tuple(rest)


def split2(x):
    hi = x.astype(jnp.bfloat16)
    lo = (x - hi.astype(jnp.float32)).astype(jnp.bfloat16)
    return hi, lo


def kernel(
    levels, lo_bits, n_lo, n_hi,
    x_ref, ain_hbm, aout_hbm, w_ref, dest_ref, out_ref,
    ain_ref, aout_ref, xs_ref, os_ref, first_ref, st_ref, got_ref, cos_ref, sin_ref, wk_ref, split_ref, pick_ref, t_ref, r_ref, b_ref,
    send_sem, recv_sem, tsend_sem, trecv_sem, bsend_sem, brecv_sem, x_sem, o_sem, a_sem,
):
    chunks = st_ref.shape[1]
    vectors = chunks * VC
    rank = st_ref.shape[-2]
    slots = dest_ref.shape[1]
    bits = slots.bit_length() - 1
    n = n_lo * n_hi
    piece = slots // n
    orders = slot_orders(levels, bits)
    my_lo = lax.axis_index("lo")
    my_hi = lax.axis_index("hi")
    me = my_lo * n_hi + my_hi

    barrier = pltpu.get_barrier_semaphore()

    def fetch(tile):
        cols = pl.ds(tile * LANES, LANES)
        return pltpu.make_async_copy(x_ref.at[:, cols], xs_ref.at[tile], x_sem.at[tile])

    for tile in range(slots // LANES):
        fetch(tile).start()

    def fetch_angles(l):
        return (
            pltpu.make_async_copy(ain_hbm.at[l], ain_ref.at[l], a_sem.at[0, l]),
            pltpu.make_async_copy(aout_hbm.at[l], aout_ref.at[l], a_sem.at[1, l]),
        )

    for l in range(levels):
        for copy in fetch_angles(l):
            copy.start()

    def greet(i, carry):
        other = lax.rem(me + i, n)
        pl.semaphore_signal(
            barrier, inc=1, device_id=(other // n_hi, lax.rem(other, n_hi)), device_id_type=MESH
        )
        return carry

    lax.fori_loop(1, n, greet, 0)

    def place(l):
        if l < lo_bits:
            axis, own, stride = "lo", my_lo, 2**l
        else:
            axis, own, stride = "hi", my_hi, 2 ** (l - lo_bits)
        side = lax.rem(own // stride, 2)
        return axis, side, own + stride * (1 - 2 * side)

    def state(l, c):
        return first_ref.at[c] if l == 0 else st_ref.at[l - 1, c]

    def exchange(l, c):
        axis, side, partner = place(l)
        where = l % TILE_BITS
        index = (slice(None),) * (2 + where) + (1 - side,)
        device = (partner, my_hi) if axis == "lo" else (my_lo, partner)
        return pltpu.make_async_remote_copy(
            src_ref=state(l, c).at[index],
            dst_ref=got_ref.at[l, c],
            send_sem=send_sem.at[l, c],
            recv_sem=recv_sem.at[l, c],
            device_id=device,
            device_id_type=MESH,
        )

    def prepare(l):
        _, side, _ = place(l)
        w = w_ref[l]
        turned = jnp.concatenate([w[:, rank:], w[:, :rank]], axis=1)
        w = jnp.where(side == 0, w, turned)
        hi, lo = split2(w)
        wk_ref[l] = jnp.concatenate([hi, hi, lo], axis=1)
        rows = 3 * rank
        for copy in fetch_angles(l):
            copy.wait()
        angle = jnp.concatenate([ain_ref[l], aout_ref[l]], axis=0)
        hi, lo = split2(angle)
        split_ref[0:rows] = hi
        split_ref[rows:2 * rows] = lo
        size = min(slots, 2 * LANES << l)

        def body(u, carry):
            wide = 2 * LANES
            if l == 0:
                tiles = (u, u + 4)
                start = u * size
            elif l == 1:
                tiles = (u // 2 + lax.rem(u, 2) * 4, u // 2 + lax.rem(u, 2) * 4 + 2)
                start = u // 2 * size
            else:
                tiles = (2 * u, 2 * u + 1)
                start = 0
            lane = lax.broadcasted_iota(jnp.int32, (1, wide), 1)
            index = jnp.where(lane < LANES, lane + tiles[0] * LANES, lane + (tiles[1] - 1) * LANES)
            source = to_logical(index, orders[l])
            ids = lax.broadcasted_iota(jnp.int32, (size, wide), 0) + start
            hot = jnp.where(ids == source, 1.0, 0.0).astype(jnp.bfloat16)
            if size == slots:
                left = split_ref[...]
            else:
                left = split_ref[:, pl.ds(pl.multiple_of(start, size), size)]
            got = jnp.dot(left, hot, preferred_element_type=jnp.float32)
            got = got[0:rows] + got[rows:2 * rows]
            sine, cosine = sincos(got)
            for half in range(2):
                cols = slice(half * LANES, (half + 1) * LANES)
                for part in range(3):
                    band = slice(part * rank, (part + 1) * rank)
                    sin_ref[l, tiles[half], part] = sine[band, cols]
                    cos_ref[l, tiles[half], part] = cosine[band, cols]
            return carry

        lax.fori_loop(0, slots // (2 * LANES), body, 0)

    def prepare_pick():
        ids = lax.broadcasted_iota(jnp.int32, (LANES, LANES), 1).astype(jnp.float32)

        for g in range(slots // LANES):
            rows = slice(g * LANES, (g + 1) * LANES)
            want = to_internal(dest_ref[:, rows], orders[levels - 1]).astype(jnp.float32)
            want = jnp.broadcast_to(want, (LANES, LANES)).T

            for u in range(slots // LANES):
                hot = jnp.where(ids + float(u * LANES) == want, 1.0, 0.0)
                pick_ref[u, rows] = hot.astype(jnp.bfloat16)

    def load_first(c):
        for v in range(VC):
            for part in range(2):
                rows = pl.ds(part * rank * vectors + c * VC + v, rank, stride=vectors)
                for tile in range(slots // LANES):
                    first_ref[c, v, part, tile // 4, tile // 2 % 2, tile % 2] = xs_ref[tile, rows, :]

    def compute(l, c):
        _, side, _ = place(l)
        src = state(l, c)

        def body(u, carry):
            a, b = u // 2, lax.rem(u, 2)
            kept = at_tile(l, side, a, b)
            kre = [src[(v, 0) + kept] for v in range(VC)]
            kim = [src[(v, 1) + kept] for v in range(VC)]
            gre = [got_ref[l, c, v, 0, a, b] for v in range(VC)]
            gim = [got_ref[l, c, v, 1, a, b] for v in range(VC)]
            columns = []
            tiles = []
            for bit in range(2):
                t9, t8, t7 = at_tile(l, bit, a, b)
                tile = t9 * 4 + t8 * 2 + t7
                tiles.append(tile)
                ck, sk = cos_ref[l, tile, side], sin_ref[l, tile, side]
                cg, sg = cos_ref[l, tile, 1 - side], sin_ref[l, tile, 1 - side]
                for v in range(VC):
                    columns.append(jnp.concatenate(
                        [kre[v] * ck - kim[v] * sk, gre[v] * cg - gim[v] * sg], axis=0))
                    columns.append(jnp.concatenate(
                        [kre[v] * sk + kim[v] * ck, gre[v] * sg + gim[v] * cg], axis=0))
            hi, lo = split2(jnp.concatenate(columns, axis=1))
            stacked = jnp.concatenate([hi, lo, hi], axis=0)
            mapped = jnp.dot(wk_ref[l], stacked, preferred_element_type=jnp.float32)
            for bit in range(2):
                co, so = cos_ref[l, tiles[bit], 2], sin_ref[l, tiles[bit], 2]
                where = at_tile(l, bit, a, b)
                for v in range(VC):
                    at = (bit * VC + v) * 2 * LANES
                    mre = mapped[:, at:at + LANES]
                    mim = mapped[:, at + LANES:at + 2 * LANES]
                    st_ref[(l, c, v, 0) + where] = mre * co - mim * so
                    st_ref[(l, c, v, 1) + where] = mre * so + mim * co
            return carry

        lax.fori_loop(0, 4, body, 0, unroll=2)

    def swap(l, c):
        lane_bit = bits - 1 - l
        shift = 2**lane_bit
        lane = lax.broadcasted_iota(jnp.int32, (rank, LANES), 1)
        clear = ((lane >> lane_bit) & 1) == 0

        def body(u, carry):
            a, b = u // 2, lax.rem(u, 2)
            first, second = at_tile(l, 0, a, b), at_tile(l, 1, a, b)
            for v in range(VC):
                for part in range(2):
                    x = st_ref[(l - 1, c, v, part) + first]
                    y = st_ref[(l - 1, c, v, part) + second]
                    st_ref[(l - 1, c, v, part) + first] = jnp.where(clear, x, pltpu.roll(y, shift, 1))
                    st_ref[(l - 1, c, v, part) + second] = jnp.where(
                        clear, pltpu.roll(x, LANES - shift, 1), y)
            return carry

        lax.fori_loop(0, 4, body, 0)

    half = n_hi // 2
    mine_half = my_hi // half
    within = lax.rem(my_hi, half)
    opposite = lax.rem(my_hi + half, n_hi)

    def rows_of(owner):
        return pl.ds(pl.multiple_of(owner * piece, piece), piece)

    def bulk(c, k):
        to_lo = lax.rem(my_lo + k + 1, n_lo)
        start = (to_lo * n_hi + (1 - mine_half) * half) * piece
        size = half * piece
        return pltpu.make_async_remote_copy(
            src_ref=t_ref.at[c, pl.ds(pl.multiple_of(start, size), size)],
            dst_ref=b_ref.at[c, to_lo],
            send_sem=bsend_sem.at[c, k],
            recv_sem=brecv_sem.at[c, k],
            device_id=(my_lo, opposite),
            device_id_type=MESH,
        )

    def offsets(i):
        return lax.rem(i // half + 1, n_lo), lax.rem(lax.rem(i, half) + 1, half)

    def relay(c, kind, i):
        off_lo, off_hi = offsets(i)
        to_lo, to_in = lax.rem(my_lo + off_lo, n_lo), lax.rem(within + off_hi, half)
        to_hi = mine_half * half + to_in
        if kind == 0:
            src = t_ref.at[c, rows_of(to_lo * n_hi + to_hi)]
            dst = r_ref.at[c, rows_of(me)]
        else:
            src = b_ref.at[c, to_lo, rows_of(to_in)]
            dst = r_ref.at[c, rows_of(my_lo * n_hi + opposite)]
        return pltpu.make_async_remote_copy(
            src_ref=src,
            dst_ref=dst,
            send_sem=tsend_sem.at[c, kind, i],
            recv_sem=trecv_sem.at[c, kind, i],
            device_id=(to_lo, to_hi),
            device_id_type=MESH,
        )

    def relay_in(c, kind, i):
        off_lo, off_hi = offsets(i)
        to_lo = lax.rem(my_lo + n_lo - off_lo, n_lo)
        to_hi = mine_half * half + lax.rem(within + half - off_hi, half)
        source = to_lo * n_hi + (to_hi if kind == 0 else lax.rem(to_hi + half, n_hi))
        return pltpu.make_async_remote_copy(
            src_ref=t_ref.at[c, rows_of(source)],
            dst_ref=r_ref.at[c, rows_of(source)],
            send_sem=tsend_sem.at[c, kind, i],
            recv_sem=trecv_sem.at[c, kind, i],
            device_id=(to_lo, to_hi),
            device_id_type=MESH,
        )

    def gather(c):
        his, los = [], []
        total = None
        for tile in range(slots // LANES):
            where = (tile // 4, tile // 2 % 2, tile % 2)
            block = jnp.concatenate(
                [st_ref[(levels - 1, PAIR * c + v, 0, part) + where] for v in range(PAIR) for part in range(2)], axis=0)
            hi, lo = split2(block)
            his.append(jnp.concatenate([hi, lo], axis=0))
        both = jnp.concatenate(his, axis=1)
        split_at = both.shape[0] // 2

        def body(u, carry):
            rows = slots // 4
            at = pl.ds(pl.multiple_of(u * rows, rows), rows)
            hot = jnp.concatenate([pick_ref[t, at] for t in range(slots // LANES)], axis=1)
            got = lax.dot_general(
                hot, both, (((1,), (1,)), ((), ())), preferred_element_type=jnp.float32)
            t_ref[c, at] = got[:, :split_at] + got[:, split_at:]
            return carry

        lax.fori_loop(0, 4, body, 0)
        for k in range(n_lo):
            bulk(c, k).start()
        r_ref[c, rows_of(me)] = t_ref[c, rows_of(me)]

        def send(i, carry):
            relay(c, 0, i).start()
            return carry

        lax.fori_loop(0, n // 2 - 1, send, 0)

    def forward(c):
        def send(i, carry):
            relay(c, 1, i).start()
            return carry

        for k in range(n_lo):
            bulk(c, k).wait_recv()
            lax.fori_loop(k * half, min((k + 1) * half, n // 2 - 1), send, 0)
        r_ref[c, rows_of(my_lo * n_hi + opposite)] = b_ref[c, my_lo, rows_of(within)]

    def put(tile):
        cols = pl.ds(tile * LANES, LANES)
        return pltpu.make_async_copy(os_ref.at[tile], out_ref.at[:, cols], o_sem.at[tile])

    def finish(c):
        def wait(i, carry):
            relay_in(c, 0, i).wait_recv()
            relay_in(c, 1, i).wait_recv()
            return carry

        lax.fori_loop(0, n // 2 - 1, wait, 0)
        for g in range(slots // LANES):
            cols = slice(g * LANES, (g + 1) * LANES)
            block = r_ref[c, cols].T
            for v in range(PAIR):
                for part in range(2):
                    at = (v * 2 + part) * rank
                    rows = pl.ds(part * rank * vectors + c * PAIR + v, rank, stride=vectors)
                    os_ref[g, rows, :] = block[at:at + rank]
            if c == chunks // PAIR - 1:
                put(g).start()

    for tile in range(slots // LANES):
        fetch(tile).wait()
    load_first(0)
    pl.semaphore_wait(barrier, n - 1)
    exchange(0, 0).start()
    for c in range(1, AHEAD):
        load_first(c)
        exchange(0, c).start()
    prepared = set()

    def need(l):
        if l < levels and l not in prepared:
            prepared.add(l)
            prepare(l)

    need(0)
    last = levels - 1
    order = sorted(
        ((c, l) for c in range(chunks) for l in range(levels)),
        key=lambda t: (t[0] + t[1] if t[1] < last else t[1] + 2 * t[0] + 1.5, -t[1]),
    )
    for c, l in order:
        need(l)
        exchange(l, c).wait_recv()
        compute(l, c)
        if l == 0 and c + AHEAD < chunks:
            load_first(c + AHEAD)
            exchange(0, c + AHEAD).start()
        if l < last:
            if l + 1 >= TILE_BITS:
                swap(l + 1, c)
            exchange(l + 1, c).start()
            need(l + 1)
            if l + 1 == last and c == 0:
                prepare_pick()
        elif c % PAIR == PAIR - 1:
            gather(c // PAIR)
            if c // PAIR >= 2:
                forward(c // PAIR - 2)
    for c in range(max(0, chunks // PAIR - 2), chunks // PAIR):
        forward(c)
    for c in range(chunks // PAIR):
        finish(c)
    for tile in range(slots // LANES):
        put(tile).wait()
    for c in range(chunks):
        for l in range(levels):
            exchange(l, c).wait_send()
    for c in range(chunks // PAIR):

        def sent(i, carry):
            relay(c, 0, i).wait_send()
            relay(c, 1, i).wait_send()
            return carry

        lax.fori_loop(0, n // 2 - 1, sent, 0)
        for k in range(n_lo):
            bulk(c, k).wait_send()


def shards(coefficients, angle_in, angle_out, interp, destination):
    parts, rank, vectors, slots = coefficients.shape
    levels = interp.shape[0]
    n_lo, n_hi = lax.axis_size("lo"), lax.axis_size("hi")
    n = n_lo * n_hi
    chunks = vectors // VC
    pairs = vectors // PAIR
    rows = PAIR * parts * rank
    vmem = pl.BlockSpec(memory_space=pltpu.VMEM)
    f32, bf16 = jnp.float32, jnp.bfloat16
    tiles = slots // LANES
    out = pl.pallas_call(
        functools.partial(kernel, levels, n_lo.bit_length() - 1, n_lo, n_hi),
        out_shape=jax.ShapeDtypeStruct((parts * rank * vectors, slots), f32),
        in_specs=[pl.BlockSpec(memory_space=pl.ANY)] * 3 + [vmem] * 2,
        out_specs=pl.BlockSpec(memory_space=pl.ANY),
        scratch_shapes=[
            pltpu.VMEM((levels, 2 * rank, slots), f32),
            pltpu.VMEM((levels, rank, slots), f32),
            pltpu.VMEM((tiles, parts * rank * vectors, LANES), f32),
            pltpu.VMEM((tiles, parts * rank * vectors, LANES), f32),
            pltpu.VMEM((chunks, VC, parts, 2, 2, 2, rank, LANES), f32),
            pltpu.VMEM((levels, chunks, VC, parts, 2, 2, 2, rank, LANES), f32),
            pltpu.VMEM((levels, chunks, VC, parts, 2, 2, rank, LANES), f32),
            pltpu.VMEM((levels, tiles, 3, rank, LANES), f32),
            pltpu.VMEM((levels, tiles, 3, rank, LANES), f32),
            pltpu.VMEM((levels, rank, 6 * rank), bf16),
            pltpu.VMEM((6 * rank, slots), bf16),
            pltpu.VMEM((tiles, slots, LANES), bf16),
            pltpu.VMEM((pairs, slots, rows), f32),
            pltpu.VMEM((pairs, slots, rows), f32),
            pltpu.VMEM((pairs, n_lo, slots // n_lo // 2, rows), f32),
            pltpu.SemaphoreType.DMA((levels, chunks)),
            pltpu.SemaphoreType.DMA((levels, chunks)),
            pltpu.SemaphoreType.DMA((pairs, 2, n // 2)),
            pltpu.SemaphoreType.DMA((pairs, 2, n // 2)),
            pltpu.SemaphoreType.DMA((pairs, n_lo)),
            pltpu.SemaphoreType.DMA((pairs, n_lo)),
            pltpu.SemaphoreType.DMA((tiles,)),
            pltpu.SemaphoreType.DMA((tiles,)),
            pltpu.SemaphoreType.DMA((2, levels)),
        ],
        compiler_params=pltpu.CompilerParams(
            collective_id=0, has_side_effects=True, vmem_limit_bytes=56 * 1024 * 1024
        ),
    )(coefficients.reshape(-1, slots), angle_in, angle_out, interp, destination)
    return out.reshape(parts, rank, vectors, slots)


def solution(mesh):
    placed = (
        P(None, None, None, ("lo", "hi")),
        P(None, None, ("lo", "hi")),
        P(None, None, ("lo", "hi")),
        P(),
        P(("lo", "hi"), None),
    )
    return jax.shard_map(
        shards,
        mesh=mesh,
        in_specs=placed,
        out_specs=P(None, None, None, ("lo", "hi")),
        check_vma=False,
    )
```

```python
import functools

import jax
import jax.numpy as jnp
from jax import lax
from jax.experimental import pallas as pl
from jax.experimental.pallas import tpu as pltpu
from jax.sharding import PartitionSpec as P

MESH = pl.DeviceIdType.MESH
LANES = 128
VC = 1
PAIR = 2
AHEAD = 4
TILE_BITS = 3


def slot_orders(levels, bits):
    lay = {q: ("k", q) for q in range(bits)}
    orders = []
    for l in range(levels):
        tile = bits - 1 - l % TILE_BITS
        lane = bits - 1 - l
        if l >= TILE_BITS:
            lay[tile], lay[lane] = lay[lane], lay[tile]
        assert lay[tile] == ("k", bits - 1 - l)
        lay[tile] = ("b", l)
        order = {}
        for q, (kind, n) in lay.items():
            order[q] = n + l + 1 if kind == "k" else l - n
        orders.append(order)
    return orders


def to_logical(index, order):
    out = jnp.zeros_like(index)
    for q, p in order.items():
        out = out | (((index >> q) & 1) << p)
    return out


def to_internal(index, order):
    out = jnp.zeros_like(index)
    for q, p in order.items():
        out = out | (((index >> p) & 1) << q)
    return out


def sincos(x):
    y = 0.5 * x
    z = y * y
    s = -1.0 / 39916800
    for c in (1.0 / 362880, -1.0 / 5040, 1.0 / 120, -1.0 / 6, 1.0):
        s = s * z + c
    s = s * y
    c = 1.0 / 479001600
    for k in (-1.0 / 3628800, 1.0 / 40320, -1.0 / 720, 1.0 / 24, -0.5, 1.0):
        c = c * z + k
    return 2.0 * s * c, 1.0 - 2.0 * s * s


def at_tile(l, value, a, b):
    where = l % TILE_BITS
    rest = [a, b]
    rest.insert(where, value)
    return tuple(rest)


def split2(x):
    hi = x.astype(jnp.bfloat16)
    lo = (x - hi.astype(jnp.float32)).astype(jnp.bfloat16)
    return hi, lo


def kernel(
    levels, lo_bits, n_lo, n_hi,
    x_ref, ain_hbm, aout_hbm, w_ref, dest_ref, out_ref,
    ain_ref, aout_ref, xs_ref, os_ref, first_ref, st_ref, got_ref, cos_ref, sin_ref, wk_ref, split_ref, pick_ref, t_ref, r_ref,
    send_sem, recv_sem, tsend_sem, trecv_sem, x_sem, o_sem, a_sem,
):
    chunks = st_ref.shape[1]
    vectors = chunks * VC
    rank = st_ref.shape[-2]
    slots = dest_ref.shape[1]
    bits = slots.bit_length() - 1
    n = n_lo * n_hi
    piece = slots // n
    orders = slot_orders(levels, bits)
    my_lo = lax.axis_index("lo")
    my_hi = lax.axis_index("hi")
    me = my_lo * n_hi + my_hi

    barrier = pltpu.get_barrier_semaphore()

    def fetch(tile):
        cols = pl.ds(tile * LANES, LANES)
        return pltpu.make_async_copy(x_ref.at[:, cols], xs_ref.at[tile], x_sem.at[tile])

    for tile in range(slots // LANES):
        fetch(tile).start()

    def fetch_angles(l):
        return (
            pltpu.make_async_copy(ain_hbm.at[l], ain_ref.at[l], a_sem.at[0, l]),
            pltpu.make_async_copy(aout_hbm.at[l], aout_ref.at[l], a_sem.at[1, l]),
        )

    for l in range(levels):
        for copy in fetch_angles(l):
            copy.start()

    def greet(i, carry):
        other = lax.rem(me + i, n)
        pl.semaphore_signal(
            barrier, inc=1, device_id=(other // n_hi, lax.rem(other, n_hi)), device_id_type=MESH
        )
        return carry

    lax.fori_loop(1, n, greet, 0)

    def place(l):
        if l < lo_bits:
            axis, own, stride = "lo", my_lo, 2**l
        else:
            axis, own, stride = "hi", my_hi, 2 ** (l - lo_bits)
        side = lax.rem(own // stride, 2)
        return axis, side, own + stride * (1 - 2 * side)

    def state(l, c):
        return first_ref.at[c] if l == 0 else st_ref.at[l - 1, c]

    def exchange(l, c):
        axis, side, partner = place(l)
        where = l % TILE_BITS
        index = (slice(None),) * (2 + where) + (1 - side,)
        device = (partner, my_hi) if axis == "lo" else (my_lo, partner)
        return pltpu.make_async_remote_copy(
            src_ref=state(l, c).at[index],
            dst_ref=got_ref.at[l, c],
            send_sem=send_sem.at[l, c],
            recv_sem=recv_sem.at[l, c],
            device_id=device,
            device_id_type=MESH,
        )

    def prepare(l):
        _, side, _ = place(l)
        w = w_ref[l]
        turned = jnp.concatenate([w[:, rank:], w[:, :rank]], axis=1)
        w = jnp.where(side == 0, w, turned)
        hi, lo = split2(w)
        wk_ref[l] = jnp.concatenate([hi, hi, lo], axis=1)
        rows = 3 * rank
        for copy in fetch_angles(l):
            copy.wait()
        angle = jnp.concatenate([ain_ref[l], aout_ref[l]], axis=0)
        hi, lo = split2(angle)
        split_ref[0:rows] = hi
        split_ref[rows:2 * rows] = lo
        size = min(slots, 2 * LANES << l)

        def body(u, carry):
            wide = 2 * LANES
            if l == 0:
                tiles = (u, u + 4)
                start = u * size
            elif l == 1:
                tiles = (u // 2 + lax.rem(u, 2) * 4, u // 2 + lax.rem(u, 2) * 4 + 2)
                start = u // 2 * size
            else:
                tiles = (2 * u, 2 * u + 1)
                start = 0
            lane = lax.broadcasted_iota(jnp.int32, (1, wide), 1)
            index = jnp.where(lane < LANES, lane + tiles[0] * LANES, lane + (tiles[1] - 1) * LANES)
            source = to_logical(index, orders[l])
            ids = lax.broadcasted_iota(jnp.int32, (size, wide), 0) + start
            hot = jnp.where(ids == source, 1.0, 0.0).astype(jnp.bfloat16)
            if size == slots:
                left = split_ref[...]
            else:
                left = split_ref[:, pl.ds(pl.multiple_of(start, size), size)]
            got = jnp.dot(left, hot, preferred_element_type=jnp.float32)
            got = got[0:rows] + got[rows:2 * rows]
            sine, cosine = sincos(got)
            for half in range(2):
                cols = slice(half * LANES, (half + 1) * LANES)
                for part in range(3):
                    band = slice(part * rank, (part + 1) * rank)
                    sin_ref[l, tiles[half], part] = sine[band, cols]
                    cos_ref[l, tiles[half], part] = cosine[band, cols]
            return carry

        lax.fori_loop(0, slots // (2 * LANES), body, 0)

    def prepare_pick():
        ids = lax.broadcasted_iota(jnp.int32, (LANES, LANES), 1).astype(jnp.float32)

        for g in range(slots // LANES):
            rows = slice(g * LANES, (g + 1) * LANES)
            want = to_internal(dest_ref[:, rows], orders[levels - 1]).astype(jnp.float32)
            want = jnp.broadcast_to(want, (LANES, LANES)).T

            for u in range(slots // LANES):
                hot = jnp.where(ids + float(u * LANES) == want, 1.0, 0.0)
                pick_ref[u, rows] = hot.astype(jnp.bfloat16)

    def load_first(c):
        for v in range(VC):
            for part in range(2):
                rows = pl.ds(part * rank * vectors + c * VC + v, rank, stride=vectors)
                for tile in range(slots // LANES):
                    first_ref[c, v, part, tile // 4, tile // 2 % 2, tile % 2] = xs_ref[tile, rows, :]

    def compute(l, c):
        _, side, _ = place(l)
        src = state(l, c)

        def body(u, carry):
            a, b = u // 2, lax.rem(u, 2)
            kept = at_tile(l, side, a, b)
            kre = [src[(v, 0) + kept] for v in range(VC)]
            kim = [src[(v, 1) + kept] for v in range(VC)]
            gre = [got_ref[l, c, v, 0, a, b] for v in range(VC)]
            gim = [got_ref[l, c, v, 1, a, b] for v in range(VC)]
            columns = []
            tiles = []
            for bit in range(2):
                t9, t8, t7 = at_tile(l, bit, a, b)
                tile = t9 * 4 + t8 * 2 + t7
                tiles.append(tile)
                ck, sk = cos_ref[l, tile, side], sin_ref[l, tile, side]
                cg, sg = cos_ref[l, tile, 1 - side], sin_ref[l, tile, 1 - side]
                for v in range(VC):
                    columns.append(jnp.concatenate(
                        [kre[v] * ck - kim[v] * sk, gre[v] * cg - gim[v] * sg], axis=0))
                    columns.append(jnp.concatenate(
                        [kre[v] * sk + kim[v] * ck, gre[v] * sg + gim[v] * cg], axis=0))
            hi, lo = split2(jnp.concatenate(columns, axis=1))
            stacked = jnp.concatenate([hi, lo, hi], axis=0)
            mapped = jnp.dot(wk_ref[l], stacked, preferred_element_type=jnp.float32)
            for bit in range(2):
                co, so = cos_ref[l, tiles[bit], 2], sin_ref[l, tiles[bit], 2]
                where = at_tile(l, bit, a, b)
                for v in range(VC):
                    at = (bit * VC + v) * 2 * LANES
                    mre = mapped[:, at:at + LANES]
                    mim = mapped[:, at + LANES:at + 2 * LANES]
                    st_ref[(l, c, v, 0) + where] = mre * co - mim * so
                    st_ref[(l, c, v, 1) + where] = mre * so + mim * co
            return carry

        lax.fori_loop(0, 4, body, 0, unroll=2)

    def swap(l, c):
        lane_bit = bits - 1 - l
        shift = 2**lane_bit
        lane = lax.broadcasted_iota(jnp.int32, (rank, LANES), 1)
        clear = ((lane >> lane_bit) & 1) == 0

        def body(u, carry):
            a, b = u // 2, lax.rem(u, 2)
            first, second = at_tile(l, 0, a, b), at_tile(l, 1, a, b)
            for v in range(VC):
                for part in range(2):
                    x = st_ref[(l - 1, c, v, part) + first]
                    y = st_ref[(l - 1, c, v, part) + second]
                    st_ref[(l - 1, c, v, part) + first] = jnp.where(clear, x, pltpu.roll(y, shift, 1))
                    st_ref[(l - 1, c, v, part) + second] = jnp.where(
                        clear, pltpu.roll(x, LANES - shift, 1), y)
            return carry

        lax.fori_loop(0, 4, body, 0)

    def offsets(i):
        half = n_hi // 2
        pair = i // 2
        off_hi = half - 1 - pair // n_lo + half * (1 - lax.rem(i, 2))
        return lax.rem(lax.rem(pair, n_lo) + 1, n_lo), lax.rem(off_hi, n_hi)

    def relay(c, i):
        off_lo, off_hi = offsets(i)
        to_lo, to_hi = lax.rem(my_lo + off_lo, n_lo), lax.rem(my_hi + off_hi, n_hi)
        other = to_lo * n_hi + to_hi
        return pltpu.make_async_remote_copy(
            src_ref=t_ref.at[c, pl.ds(pl.multiple_of(other * piece, piece), piece)],
            dst_ref=r_ref.at[c, pl.ds(pl.multiple_of(me * piece, piece), piece)],
            send_sem=tsend_sem.at[c, i],
            recv_sem=trecv_sem.at[c, i],
            device_id=(to_lo, to_hi),
            device_id_type=MESH,
        )

    def relay_in(c, i):
        off_lo, off_hi = offsets(i)
        to_lo = lax.rem(my_lo + n_lo - off_lo, n_lo)
        to_hi = lax.rem(my_hi + n_hi - off_hi, n_hi)
        other = to_lo * n_hi + to_hi
        return pltpu.make_async_remote_copy(
            src_ref=t_ref.at[c, pl.ds(pl.multiple_of(other * piece, piece), piece)],
            dst_ref=r_ref.at[c, pl.ds(pl.multiple_of(other * piece, piece), piece)],
            send_sem=tsend_sem.at[c, i],
            recv_sem=trecv_sem.at[c, i],
            device_id=(to_lo, to_hi),
            device_id_type=MESH,
        )

    def gather(c):
        his, los = [], []
        total = None
        for tile in range(slots // LANES):
            where = (tile // 4, tile // 2 % 2, tile % 2)
            block = jnp.concatenate(
                [st_ref[(levels - 1, PAIR * c + v, 0, part) + where] for v in range(PAIR) for part in range(2)], axis=0)
            hi, lo = split2(block)
            his.append(jnp.concatenate([hi, lo], axis=0))
        both = jnp.concatenate(his, axis=1)
        split_at = both.shape[0] // 2

        def body(u, carry):
            rows = slots // 4
            at = pl.ds(pl.multiple_of(u * rows, rows), rows)
            hot = jnp.concatenate([pick_ref[t, at] for t in range(slots // LANES)], axis=1)
            got = lax.dot_general(
                hot, both, (((1,), (1,)), ((), ())), preferred_element_type=jnp.float32)
            t_ref[c, at] = got[:, :split_at] + got[:, split_at:]
            return carry

        lax.fori_loop(0, 4, body, 0)
        mine = pl.ds(pl.multiple_of(me * piece, piece), piece)
        r_ref[c, mine] = t_ref[c, mine]

        def send(i, carry):
            relay(c, i).start()
            return carry

        lax.fori_loop(0, n - 1, send, 0)

    def put(tile):
        cols = pl.ds(tile * LANES, LANES)
        return pltpu.make_async_copy(os_ref.at[tile], out_ref.at[:, cols], o_sem.at[tile])

    def finish(c):
        def wait(i, carry):
            relay_in(c, i).wait_recv()
            return carry

        lax.fori_loop(0, n - 1, wait, 0)
        for g in range(slots // LANES):
            cols = slice(g * LANES, (g + 1) * LANES)
            block = r_ref[c, cols].T
            for v in range(PAIR):
                for part in range(2):
                    at = (v * 2 + part) * rank
                    rows = pl.ds(part * rank * vectors + c * PAIR + v, rank, stride=vectors)
                    os_ref[g, rows, :] = block[at:at + rank]
            if c == chunks // PAIR - 1:
                put(g).start()

    for tile in range(slots // LANES):
        fetch(tile).wait()
    load_first(0)
    pl.semaphore_wait(barrier, n - 1)
    exchange(0, 0).start()
    for c in range(1, AHEAD):
        load_first(c)
        exchange(0, c).start()
    prepared = set()

    def need(l):
        if l < levels and l not in prepared:
            prepared.add(l)
            prepare(l)

    need(0)
    need(1)
    last = levels - 1
    order = sorted(
        ((c, l) for c in range(chunks) for l in range(levels)),
        key=lambda t: (t[0] + t[1] if t[1] < last else t[1] + 2 * t[0] + 1.5, -t[1]),
    )
    for c, l in order:
        need(l)
        exchange(l, c).wait_recv()
        compute(l, c)
        if l == 0 and c + AHEAD < chunks:
            load_first(c + AHEAD)
            exchange(0, c + AHEAD).start()
        if l < last:
            if l + 1 >= TILE_BITS:
                swap(l + 1, c)
            exchange(l + 1, c).start()
            if l == 0:
                need(2)
            elif l >= 2:
                need(l + 1)
            if l + 1 == last and c == 0:
                prepare_pick()
        elif c % PAIR == PAIR - 1:
            gather(c // PAIR)
    for c in range(chunks // PAIR):
        finish(c)
    for tile in range(slots // LANES):
        put(tile).wait()
    for c in range(chunks):
        for l in range(levels):
            exchange(l, c).wait_send()
    for c in range(chunks // PAIR):

        def sent(i, carry):
            relay(c, i).wait_send()
            return carry

        lax.fori_loop(0, n - 1, sent, 0)


def shards(coefficients, angle_in, angle_out, interp, destination):
    parts, rank, vectors, slots = coefficients.shape
    levels = interp.shape[0]
    n_lo, n_hi = lax.axis_size("lo"), lax.axis_size("hi")
    n = n_lo * n_hi
    chunks = vectors // VC
    pairs = vectors // PAIR
    rows = PAIR * parts * rank
    vmem = pl.BlockSpec(memory_space=pltpu.VMEM)
    f32, bf16 = jnp.float32, jnp.bfloat16
    tiles = slots // LANES
    out = pl.pallas_call(
        functools.partial(kernel, levels, n_lo.bit_length() - 1, n_lo, n_hi),
        out_shape=jax.ShapeDtypeStruct((parts * rank * vectors, slots), f32),
        in_specs=[pl.BlockSpec(memory_space=pl.ANY)] * 3 + [vmem] * 2,
        out_specs=pl.BlockSpec(memory_space=pl.ANY),
        scratch_shapes=[
            pltpu.VMEM((levels, 2 * rank, slots), f32),
            pltpu.VMEM((levels, rank, slots), f32),
            pltpu.VMEM((tiles, parts * rank * vectors, LANES), f32),
            pltpu.VMEM((tiles, parts * rank * vectors, LANES), f32),
            pltpu.VMEM((chunks, VC, parts, 2, 2, 2, rank, LANES), f32),
            pltpu.VMEM((levels, chunks, VC, parts, 2, 2, 2, rank, LANES), f32),
            pltpu.VMEM((levels, chunks, VC, parts, 2, 2, rank, LANES), f32),
            pltpu.VMEM((levels, tiles, 3, rank, LANES), f32),
            pltpu.VMEM((levels, tiles, 3, rank, LANES), f32),
            pltpu.VMEM((levels, rank, 6 * rank), bf16),
            pltpu.VMEM((6 * rank, slots), bf16),
            pltpu.VMEM((tiles, slots, LANES), bf16),
            pltpu.VMEM((pairs, slots, rows), f32),
            pltpu.VMEM((pairs, slots, rows), f32),
            pltpu.SemaphoreType.DMA((levels, chunks)),
            pltpu.SemaphoreType.DMA((levels, chunks)),
            pltpu.SemaphoreType.DMA((pairs, n)),
            pltpu.SemaphoreType.DMA((pairs, n)),
            pltpu.SemaphoreType.DMA((tiles,)),
            pltpu.SemaphoreType.DMA((tiles,)),
            pltpu.SemaphoreType.DMA((2, levels)),
        ],
        compiler_params=pltpu.CompilerParams(
            collective_id=0, has_side_effects=True, vmem_limit_bytes=56 * 1024 * 1024
        ),
    )(coefficients.reshape(-1, slots), angle_in, angle_out, interp, destination)
    return out.reshape(parts, rank, vectors, slots)


def solution(mesh):
    placed = (
        P(None, None, None, ("lo", "hi")),
        P(None, None, ("lo", "hi")),
        P(None, None, ("lo", "hi")),
        P(),
        P(("lo", "hi"), None),
    )
    return jax.shard_map(
        shards,
        mesh=mesh,
        in_specs=placed,
        out_specs=P(None, None, None, ("lo", "hi")),
        check_vma=False,
    )
```

```python
import functools

import jax
import jax.numpy as jnp
from jax import lax
from jax.experimental import pallas as pl
from jax.experimental.pallas import tpu as pltpu
from jax.sharding import PartitionSpec as P

MESH = pl.DeviceIdType.MESH
LANES = 128
VC = 1
PAIR = 2
AHEAD = 4
TILE_BITS = 3


def slot_orders(levels, bits):
    lay = {q: ("k", q) for q in range(bits)}
    orders = []
    for l in range(levels):
        tile = bits - 1 - l % TILE_BITS
        lane = bits - 1 - l
        if l >= TILE_BITS:
            lay[tile], lay[lane] = lay[lane], lay[tile]
        assert lay[tile] == ("k", bits - 1 - l)
        lay[tile] = ("b", l)
        order = {}
        for q, (kind, n) in lay.items():
            order[q] = n + l + 1 if kind == "k" else l - n
        orders.append(order)
    return orders


def to_logical(index, order):
    out = jnp.zeros_like(index)
    for q, p in order.items():
        out = out | (((index >> q) & 1) << p)
    return out


def to_internal(index, order):
    out = jnp.zeros_like(index)
    for q, p in order.items():
        out = out | (((index >> p) & 1) << q)
    return out


def sincos(x):
    y = 0.5 * x
    z = y * y
    s = -1.0 / 39916800
    for c in (1.0 / 362880, -1.0 / 5040, 1.0 / 120, -1.0 / 6, 1.0):
        s = s * z + c
    s = s * y
    c = 1.0 / 479001600
    for k in (-1.0 / 3628800, 1.0 / 40320, -1.0 / 720, 1.0 / 24, -0.5, 1.0):
        c = c * z + k
    return 2.0 * s * c, 1.0 - 2.0 * s * s


def at_tile(l, value, a, b):
    where = l % TILE_BITS
    rest = [a, b]
    rest.insert(where, value)
    return tuple(rest)


def split2(x):
    hi = x.astype(jnp.bfloat16)
    lo = (x - hi.astype(jnp.float32)).astype(jnp.bfloat16)
    return hi, lo


def kernel(
    levels, lo_bits, n_lo, n_hi,
    x_ref, ain_hbm, aout_hbm, w_ref, dest_ref, out_ref,
    ain_ref, aout_ref, xs_ref, os_ref, first_ref, st_ref, got_ref, cos_ref, sin_ref, wk_ref, split_ref, pick_ref, t_ref, r_ref,
    send_sem, recv_sem, tsend_sem, trecv_sem, x_sem, o_sem, a_sem,
):
    chunks = st_ref.shape[1]
    vectors = chunks * VC
    rank = st_ref.shape[-2]
    slots = dest_ref.shape[1]
    bits = slots.bit_length() - 1
    n = n_lo * n_hi
    piece = slots // n
    orders = slot_orders(levels, bits)
    my_lo = lax.axis_index("lo")
    my_hi = lax.axis_index("hi")
    me = my_lo * n_hi + my_hi

    barrier = pltpu.get_barrier_semaphore()

    def fetch(tile):
        cols = pl.ds(tile * LANES, LANES)
        return pltpu.make_async_copy(x_ref.at[:, cols], xs_ref.at[tile], x_sem.at[tile])

    for tile in range(slots // LANES):
        fetch(tile).start()

    def fetch_angles(l):
        return (
            pltpu.make_async_copy(ain_hbm.at[l], ain_ref.at[l], a_sem.at[0, l]),
            pltpu.make_async_copy(aout_hbm.at[l], aout_ref.at[l], a_sem.at[1, l]),
        )

    for l in range(levels):
        for copy in fetch_angles(l):
            copy.start()

    def greet(i, carry):
        other = lax.rem(me + i, n)
        pl.semaphore_signal(
            barrier, inc=1, device_id=(other // n_hi, lax.rem(other, n_hi)), device_id_type=MESH
        )
        return carry

    lax.fori_loop(1, n, greet, 0)

    def place(l):
        if l < lo_bits:
            axis, own, stride = "lo", my_lo, 2**l
        else:
            axis, own, stride = "hi", my_hi, 2 ** (l - lo_bits)
        side = lax.rem(own // stride, 2)
        return axis, side, own + stride * (1 - 2 * side)

    def state(l, c):
        return first_ref.at[c] if l == 0 else st_ref.at[l - 1, c]

    def exchange(l, c):
        axis, side, partner = place(l)
        where = l % TILE_BITS
        index = (slice(None),) * (2 + where) + (1 - side,)
        device = (partner, my_hi) if axis == "lo" else (my_lo, partner)
        return pltpu.make_async_remote_copy(
            src_ref=state(l, c).at[index],
            dst_ref=got_ref.at[l, c],
            send_sem=send_sem.at[l, c],
            recv_sem=recv_sem.at[l, c],
            device_id=device,
            device_id_type=MESH,
        )

    def prepare(l):
        _, side, _ = place(l)
        w = w_ref[l]
        turned = jnp.concatenate([w[:, rank:], w[:, :rank]], axis=1)
        w = jnp.where(side == 0, w, turned)
        hi, lo = split2(w)
        wk_ref[l] = jnp.concatenate([hi, hi, lo], axis=1)
        rows = 3 * rank
        for copy in fetch_angles(l):
            copy.wait()
        angle = jnp.concatenate([ain_ref[l], aout_ref[l]], axis=0)
        hi, lo = split2(angle)
        split_ref[0:rows] = hi
        split_ref[rows:2 * rows] = lo
        size = min(slots, 2 * LANES << l)

        def body(u, carry):
            wide = 2 * LANES
            if l == 0:
                tiles = (u, u + 4)
                start = u * size
            elif l == 1:
                tiles = (u // 2 + lax.rem(u, 2) * 4, u // 2 + lax.rem(u, 2) * 4 + 2)
                start = u // 2 * size
            else:
                tiles = (2 * u, 2 * u + 1)
                start = 0
            lane = lax.broadcasted_iota(jnp.int32, (1, wide), 1)
            index = jnp.where(lane < LANES, lane + tiles[0] * LANES, lane + (tiles[1] - 1) * LANES)
            source = to_logical(index, orders[l])
            ids = lax.broadcasted_iota(jnp.int32, (size, wide), 0) + start
            hot = jnp.where(ids == source, 1.0, 0.0).astype(jnp.bfloat16)
            if size == slots:
                left = split_ref[...]
            else:
                left = split_ref[:, pl.ds(pl.multiple_of(start, size), size)]
            got = jnp.dot(left, hot, preferred_element_type=jnp.float32)
            got = got[0:rows] + got[rows:2 * rows]
            sine, cosine = sincos(got)
            for half in range(2):
                cols = slice(half * LANES, (half + 1) * LANES)
                for part in range(3):
                    band = slice(part * rank, (part + 1) * rank)
                    sin_ref[l, tiles[half], part] = sine[band, cols]
                    cos_ref[l, tiles[half], part] = cosine[band, cols]
            return carry

        lax.fori_loop(0, slots // (2 * LANES), body, 0)

    def prepare_pick():
        ids = lax.broadcasted_iota(jnp.int32, (LANES, LANES), 1).astype(jnp.float32)

        for g in range(slots // LANES):
            rows = slice(g * LANES, (g + 1) * LANES)
            want = to_internal(dest_ref[:, rows], orders[levels - 1]).astype(jnp.float32)
            want = jnp.broadcast_to(want, (LANES, LANES)).T

            for u in range(slots // LANES):
                hot = jnp.where(ids + float(u * LANES) == want, 1.0, 0.0)
                pick_ref[u, rows] = hot.astype(jnp.bfloat16)

    def load_first(c):
        for v in range(VC):
            for part in range(2):
                rows = pl.ds(part * rank * vectors + c * VC + v, rank, stride=vectors)
                for tile in range(slots // LANES):
                    first_ref[c, v, part, tile // 4, tile // 2 % 2, tile % 2] = xs_ref[tile, rows, :]

    def compute(l, c):
        _, side, _ = place(l)
        src = state(l, c)

        def body(u, carry):
            a, b = u // 2, lax.rem(u, 2)
            kept = at_tile(l, side, a, b)
            kre = [src[(v, 0) + kept] for v in range(VC)]
            kim = [src[(v, 1) + kept] for v in range(VC)]
            gre = [got_ref[l, c, v, 0, a, b] for v in range(VC)]
            gim = [got_ref[l, c, v, 1, a, b] for v in range(VC)]
            columns = []
            tiles = []
            for bit in range(2):
                t9, t8, t7 = at_tile(l, bit, a, b)
                tile = t9 * 4 + t8 * 2 + t7
                tiles.append(tile)
                ck, sk = cos_ref[l, tile, side], sin_ref[l, tile, side]
                cg, sg = cos_ref[l, tile, 1 - side], sin_ref[l, tile, 1 - side]
                for v in range(VC):
                    columns.append(jnp.concatenate(
                        [kre[v] * ck - kim[v] * sk, gre[v] * cg - gim[v] * sg], axis=0))
                    columns.append(jnp.concatenate(
                        [kre[v] * sk + kim[v] * ck, gre[v] * sg + gim[v] * cg], axis=0))
            hi, lo = split2(jnp.concatenate(columns, axis=1))
            stacked = jnp.concatenate([hi, lo, hi], axis=0)
            mapped = jnp.dot(wk_ref[l], stacked, preferred_element_type=jnp.float32)
            for bit in range(2):
                co, so = cos_ref[l, tiles[bit], 2], sin_ref[l, tiles[bit], 2]
                where = at_tile(l, bit, a, b)
                for v in range(VC):
                    at = (bit * VC + v) * 2 * LANES
                    mre = mapped[:, at:at + LANES]
                    mim = mapped[:, at + LANES:at + 2 * LANES]
                    st_ref[(l, c, v, 0) + where] = mre * co - mim * so
                    st_ref[(l, c, v, 1) + where] = mre * so + mim * co
            return carry

        lax.fori_loop(0, 4, body, 0, unroll=2)

    def swap(l, c):
        lane_bit = bits - 1 - l
        shift = 2**lane_bit
        lane = lax.broadcasted_iota(jnp.int32, (rank, LANES), 1)
        clear = ((lane >> lane_bit) & 1) == 0

        def body(u, carry):
            a, b = u // 2, lax.rem(u, 2)
            first, second = at_tile(l, 0, a, b), at_tile(l, 1, a, b)
            for v in range(VC):
                for part in range(2):
                    x = st_ref[(l - 1, c, v, part) + first]
                    y = st_ref[(l - 1, c, v, part) + second]
                    st_ref[(l - 1, c, v, part) + first] = jnp.where(clear, x, pltpu.roll(y, shift, 1))
                    st_ref[(l - 1, c, v, part) + second] = jnp.where(
                        clear, pltpu.roll(x, LANES - shift, 1), y)
            return carry

        lax.fori_loop(0, 4, body, 0)

    half = n_hi // 2

    def peer(i, sign):
        own = i // (n // 2)
        r = lax.rem(i, n // 2)
        off_lo = lax.rem(lax.rem(r, n_lo) + 1, n_lo)
        off_in = lax.rem(r // n_lo + 1, half)
        to_lo = lax.rem(my_lo + n_lo + sign * off_lo, n_lo)
        to_in = lax.rem(lax.rem(my_hi, half) + half + sign * off_in, half)
        side = lax.rem(my_hi // half + 1 + own, 2)
        return to_lo, side * half + to_in

    def relay(c, i):
        to_lo, to_hi = peer(i, 1)
        other = to_lo * n_hi + to_hi
        return pltpu.make_async_remote_copy(
            src_ref=t_ref.at[c, pl.ds(pl.multiple_of(other * piece, piece), piece)],
            dst_ref=r_ref.at[c, pl.ds(pl.multiple_of(me * piece, piece), piece)],
            send_sem=tsend_sem.at[c, i],
            recv_sem=trecv_sem.at[c, i],
            device_id=(to_lo, to_hi),
            device_id_type=MESH,
        )

    def relay_in(c, i):
        to_lo, to_hi = peer(i, -1)
        other = to_lo * n_hi + to_hi
        return pltpu.make_async_remote_copy(
            src_ref=t_ref.at[c, pl.ds(pl.multiple_of(other * piece, piece), piece)],
            dst_ref=r_ref.at[c, pl.ds(pl.multiple_of(other * piece, piece), piece)],
            send_sem=tsend_sem.at[c, i],
            recv_sem=trecv_sem.at[c, i],
            device_id=(to_lo, to_hi),
            device_id_type=MESH,
        )

    def gather(c):
        his, los = [], []
        total = None
        for tile in range(slots // LANES):
            where = (tile // 4, tile // 2 % 2, tile % 2)
            block = jnp.concatenate(
                [st_ref[(levels - 1, PAIR * c + v, 0, part) + where] for v in range(PAIR) for part in range(2)], axis=0)
            hi, lo = split2(block)
            his.append(jnp.concatenate([hi, lo], axis=0))
        both = jnp.concatenate(his, axis=1)
        split_at = both.shape[0] // 2

        def body(u, carry):
            rows = slots // 4
            at = pl.ds(pl.multiple_of(u * rows, rows), rows)
            hot = jnp.concatenate([pick_ref[t, at] for t in range(slots // LANES)], axis=1)
            got = lax.dot_general(
                hot, both, (((1,), (1,)), ((), ())), preferred_element_type=jnp.float32)
            t_ref[c, at] = got[:, :split_at] + got[:, split_at:]
            return carry

        lax.fori_loop(0, 4, body, 0)
        mine = pl.ds(pl.multiple_of(me * piece, piece), piece)
        r_ref[c, mine] = t_ref[c, mine]

        def send(i, carry):
            relay(c, i).start()
            return carry

        lax.fori_loop(0, n - 1, send, 0)

    def put(tile):
        cols = pl.ds(tile * LANES, LANES)
        return pltpu.make_async_copy(os_ref.at[tile], out_ref.at[:, cols], o_sem.at[tile])

    def finish(c):
        def wait(i, carry):
            relay_in(c, i).wait_recv()
            return carry

        lax.fori_loop(0, n - 1, wait, 0)
        for g in range(slots // LANES):
            cols = slice(g * LANES, (g + 1) * LANES)
            block = r_ref[c, cols].T
            for v in range(PAIR):
                for part in range(2):
                    at = (v * 2 + part) * rank
                    rows = pl.ds(part * rank * vectors + c * PAIR + v, rank, stride=vectors)
                    os_ref[g, rows, :] = block[at:at + rank]
            if c == chunks // PAIR - 1:
                put(g).start()

    for tile in range(slots // LANES):
        fetch(tile).wait()
    load_first(0)
    pl.semaphore_wait(barrier, n - 1)
    exchange(0, 0).start()
    for c in range(1, AHEAD):
        load_first(c)
        exchange(0, c).start()
    prepared = set()

    def need(l):
        if l < levels and l not in prepared:
            prepared.add(l)
            prepare(l)

    need(0)
    last = levels - 1
    order = sorted(
        ((c, l) for c in range(chunks) for l in range(levels)),
        key=lambda t: (t[0] + t[1] if t[1] < last else t[1] + 2 * t[0] + 1.5, -t[1]),
    )
    for c, l in order:
        need(l)
        exchange(l, c).wait_recv()
        compute(l, c)
        if l == 0 and c + AHEAD < chunks:
            load_first(c + AHEAD)
            exchange(0, c + AHEAD).start()
        if l < last:
            if l + 1 >= TILE_BITS:
                swap(l + 1, c)
            exchange(l + 1, c).start()
            need(l + 1)
            if l + 1 == last and c == 0:
                prepare_pick()
        elif c % PAIR == PAIR - 1:
            gather(c // PAIR)
    for c in range(chunks // PAIR):
        finish(c)
    for tile in range(slots // LANES):
        put(tile).wait()
    for c in range(chunks):
        for l in range(levels):
            exchange(l, c).wait_send()
    for c in range(chunks // PAIR):

        def sent(i, carry):
            relay(c, i).wait_send()
            return carry

        lax.fori_loop(0, n - 1, sent, 0)


def shards(coefficients, angle_in, angle_out, interp, destination):
    parts, rank, vectors, slots = coefficients.shape
    levels = interp.shape[0]
    n_lo, n_hi = lax.axis_size("lo"), lax.axis_size("hi")
    n = n_lo * n_hi
    chunks = vectors // VC
    pairs = vectors // PAIR
    rows = PAIR * parts * rank
    vmem = pl.BlockSpec(memory_space=pltpu.VMEM)
    f32, bf16 = jnp.float32, jnp.bfloat16
    tiles = slots // LANES
    out = pl.pallas_call(
        functools.partial(kernel, levels, n_lo.bit_length() - 1, n_lo, n_hi),
        out_shape=jax.ShapeDtypeStruct((parts * rank * vectors, slots), f32),
        in_specs=[pl.BlockSpec(memory_space=pl.ANY)] * 3 + [vmem] * 2,
        out_specs=pl.BlockSpec(memory_space=pl.ANY),
        scratch_shapes=[
            pltpu.VMEM((levels, 2 * rank, slots), f32),
            pltpu.VMEM((levels, rank, slots), f32),
            pltpu.VMEM((tiles, parts * rank * vectors, LANES), f32),
            pltpu.VMEM((tiles, parts * rank * vectors, LANES), f32),
            pltpu.VMEM((chunks, VC, parts, 2, 2, 2, rank, LANES), f32),
            pltpu.VMEM((levels, chunks, VC, parts, 2, 2, 2, rank, LANES), f32),
            pltpu.VMEM((levels, chunks, VC, parts, 2, 2, rank, LANES), f32),
            pltpu.VMEM((levels, tiles, 3, rank, LANES), f32),
            pltpu.VMEM((levels, tiles, 3, rank, LANES), f32),
            pltpu.VMEM((levels, rank, 6 * rank), bf16),
            pltpu.VMEM((6 * rank, slots), bf16),
            pltpu.VMEM((tiles, slots, LANES), bf16),
            pltpu.VMEM((pairs, slots, rows), f32),
            pltpu.VMEM((pairs, slots, rows), f32),
            pltpu.SemaphoreType.DMA((levels, chunks)),
            pltpu.SemaphoreType.DMA((levels, chunks)),
            pltpu.SemaphoreType.DMA((pairs, n)),
            pltpu.SemaphoreType.DMA((pairs, n)),
            pltpu.SemaphoreType.DMA((tiles,)),
            pltpu.SemaphoreType.DMA((tiles,)),
            pltpu.SemaphoreType.DMA((2, levels)),
        ],
        compiler_params=pltpu.CompilerParams(
            collective_id=0, has_side_effects=True, vmem_limit_bytes=56 * 1024 * 1024
        ),
    )(coefficients.reshape(-1, slots), angle_in, angle_out, interp, destination)
    return out.reshape(parts, rank, vectors, slots)


def solution(mesh):
    placed = (
        P(None, None, None, ("lo", "hi")),
        P(None, None, ("lo", "hi")),
        P(None, None, ("lo", "hi")),
        P(),
        P(("lo", "hi"), None),
    )
    return jax.shard_map(
        shards,
        mesh=mesh,
        in_specs=placed,
        out_specs=P(None, None, None, ("lo", "hi")),
        check_vma=False,
    )
```
